1024 devices in a mesh: ens: 16 (over x, z_hi), grid: 64 (over z_lo, y, core).
Axes of the slice: x: 4, y: 4, z: 32 (z_hi: 4, z_lo: 8; z = z_hi * 8 + z_lo), core: 2. Of those that a mesh axis runs over, the one named last changes fastest.
Arguments:
- mesh_latent: bfloat16 [16, 4096, 1024], P('ens', 'grid'), may hold values from -6 to 6
- grid_latent: bfloat16 [16, 8192, 1024], P('ens', 'grid'), may hold values from -6 to 6
- edges: int32 [8192, 3], P('grid'), may hold values from 0 to 4095, as said below
- truth: float32 [100, 8192], P(None, 'grid'), may hold values from -6 to 6
- area: float32 [8192], P('grid'), may hold values from 0.3 to 3
- chan_weight: float32 [100], replicated, may hold values from 0.2 to 2
- gain: float32 [1024], replicated, may hold values from 0.5 to 1.5
- w_hidden: bfloat16 [1024, 1024], P('grid'), may hold values from -0.1875 to 0.1875
- w_out: bfloat16 [1024, 100], P('grid'), may hold values from -0.1875 to 0.1875
Outputs:
- grad_hidden: float32 [1024, 1024], P('grid')
- grad_out: float32 [1024, 100], P('grid')
- grad_gain: float32 [1024], P('grid')
- pred_grad: float32 [16, 100, 8192], P('ens', None, 'grid')
The draws below stay inside these ranges and needn't reach their ends.
Inputs may be any that keep to these rules, and one draw needn't show every extreme that they name: `edges`: grid points 128 a block and mesh nodes 64 a block: every edge of a grid point in block b names a mesh node of block b - 1, b or b + 1, counted cyclically over the blocks.
All inputs are finite; a program needn't handle non-finite values.
Results may differ from the reference program's by a relative error of at most 0.023.
Values may be sent and summed in bfloat16 or wider, within the bound.
A program may use at most 32 MiB of HBM per device.

```python
import math
import jax
import jax.numpy as jnp
from jax import lax

H = 1024
C = 100
G_DEV = 128
NM_DEV = 64
K = 3
ENS = 16
NGRID = 8192
NMESH = 4096


def draw_edges(key, part):
    key = jax.random.fold_in(key, 7)
    block = jnp.arange(NGRID, dtype=jnp.int32) // G_DEV
    offsets = jax.random.randint(key, (NGRID, K), -NM_DEV, 2 * NM_DEV, dtype=jnp.int32)
    nodes = (block[:, None] * NM_DEV + offsets) % NMESH
    nodes = nodes.at[0, 0].set(NMESH - 1)
    nodes = nodes.at[0, 1].set(0)
    return nodes.astype(jnp.int32)


def levels(stream_key, extent, pieces, least, top_value):
    factor_of, own = 1.0, jax.random.fold_in(stream_key, 6)
    for position, parts in pieces:
        steps = jnp.exp(jax.random.uniform(jax.random.fold_in(own, position), (parts,), jnp.float32, least / len(pieces), top_value / len(pieces)))
        factor_of = factor_of * jnp.repeat(steps, extent[position] // parts).reshape([-1 if axis == position else 1 for axis in range(len(extent))])
    return factor_of


def centred(stream_key, shape, spread, bound, pieces=(), kind=jnp.bfloat16):
    entries = jax.random.normal(stream_key, shape, jnp.float32) * spread
    if len(pieces) > 0:
        entries = levels(stream_key, shape, pieces, -0.22, 0.18) * entries
    return jnp.clip(entries, min=-bound, max=bound).astype(kind)


def setup_inputs(seed: int = 0) -> dict:
    keys = jax.random.split(jax.random.key(seed), 10)
    mesh_latent = centred(keys[0], (ENS, NMESH, H), 1.0, 6.0, ((0, 16), (1, 64)))
    grid_latent = centred(keys[1], (ENS, NGRID, H), 1.0, 6.0, ((0, 16), (1, 64)))
    edges = draw_edges(jax.random.fold_in(keys[9], 71), 0)
    truth = centred(keys[3], (C, NGRID), 1.0, 6.0, ((1, 64),), jnp.float32)
    area = jnp.clip(jnp.exp(math.log(3.0) - 2.3025851 * jax.random.uniform(keys[4], (NGRID,), jnp.float32) ** levels(keys[4], (NGRID,), ((0, 64),), -0.2, 0.2)), 0.3, 3.0)
    chan_weight = jnp.clip(jnp.exp(jax.random.uniform(keys[5], (C,), jnp.float32, math.log(0.2), math.log(2.0))), 0.2, 2.0)
    gain = jnp.clip(1.0 + 0.1 * jax.random.normal(keys[6], (H,), jnp.float32), 0.5, 1.5)
    w_hidden = centred(keys[7], (H, H), H ** -0.5, 0.1875, ((0, 64),))
    w_out = centred(keys[8], (H, C), H ** -0.5, 0.1875, ((0, 64),))
    return dict(mesh_latent=mesh_latent, grid_latent=grid_latent, edges=edges, truth=truth, area=area, chan_weight=chan_weight, gain=gain, w_hidden=w_hidden, w_out=w_out)


EPS_SMOOTH = 0.1
LN_EPS = 1e-05

def slope(diff):
    return diff / jnp.sqrt(diff * diff + EPS_SMOOTH * EPS_SMOOTH)

def gelu_tanh(value):
    return jax.nn.gelu(value, approximate=True)

def forward(mesh_one, grid_one, edges, gain, w_hidden, w_out):
    gathered = mesh_one[edges]
    agg = lax.optimization_barrier(jnp.sum(gathered.astype(jnp.float32), axis=1)) / K
    state = grid_one.astype(jnp.float32) + agg
    center = state - lax.optimization_barrier(jnp.mean(state, axis=-1, keepdims=True))
    var = lax.optimization_barrier(jnp.mean(center * center, axis=-1, keepdims=True))
    norm_hat = center * lax.rsqrt(var + LN_EPS)
    normed = (norm_hat * gain[None, :]).astype(jnp.bfloat16)
    pre = jnp.dot(normed, w_hidden, preferred_element_type=jnp.float32)
    act = gelu_tanh(pre).astype(jnp.bfloat16)
    pred = lax.dot_general(w_out, act, (((0,), (1,)), ((), ())), preferred_element_type=jnp.float32)
    return (pred.astype(jnp.bfloat16), norm_hat, normed, pre, act)

def reference(mesh_latent, grid_latent, edges, truth, area, chan_weight, gain, w_hidden, w_out):

    def only_pred(pair_in):
        return forward(pair_in[0], pair_in[1], edges, gain, w_hidden, w_out)[0]
    preds = lax.map(only_pred, (mesh_latent, grid_latent))
    pf = preds.astype(jnp.float32)
    pair = jnp.zeros(pf.shape, jnp.float32)
    for member in range(ENS):
        pair = pair + slope(pf - pf[member][None])
    pred_grad = area[None, None, :] * chan_weight[None, :, None] * (slope(pf - truth[None]) - pair / (ENS - 1))
    scale = 1.0 / math.sqrt(ENS * NGRID)

    def accumulate(carry, inputs):
        mesh_one, grid_one, grad_one = inputs
        pred, norm_hat, normed, pre, act = forward(mesh_one, grid_one, edges, gain, w_hidden, w_out)
        grad_b = grad_one.astype(jnp.bfloat16)
        d_act = lax.dot_general(grad_b, w_out, (((0,), (1,)), ((), ())), preferred_element_type=jnp.float32)
        d_pre = jax.vjp(gelu_tanh, pre)[1](d_act)[0].astype(jnp.bfloat16)
        d_hidden = lax.dot_general(normed, d_pre, (((0,), (0,)), ((), ())), preferred_element_type=jnp.float32)
        d_out = lax.dot_general(act, grad_b, (((0,), (1,)), ((), ())), preferred_element_type=jnp.float32)
        d_normed = lax.dot_general(d_pre, w_hidden, (((1,), (1,)), ((), ())), preferred_element_type=jnp.float32)
        d_gain = lax.optimization_barrier(jnp.sum(d_normed * norm_hat, axis=0))
        return ((carry[0] + d_hidden, carry[1] + d_out, carry[2] + d_gain), None)
    init = (jnp.zeros((H, H), jnp.float32), jnp.zeros((H, C), jnp.float32), jnp.zeros((H,), jnp.float32))
    totals, unused = lax.scan(accumulate, init, (mesh_latent, grid_latent, pred_grad))
    return (totals[0] * scale, totals[1] * scale, totals[2] * scale, pred_grad)
```

```python
import functools
import math
from typing import NamedTuple

import jax
import jax.numpy as jnp
from jax import lax
from jax.experimental import pallas as pl
from jax.experimental.pallas import tpu as pltpu
from jax.sharding import PartitionSpec as P

LN_EPS = 1e-05
F32, BF16 = jnp.float32, jnp.bfloat16
ROWS = 16
NT = (((1,), (1,)), ((), ()))


class Sizes(NamedTuple):
    x: int = 4
    y: int = 4
    zl: int = 8
    zh: int = 4
    points: int = 128
    nodes: int = 64
    chans: int = 100
    pad: int = 128
    chunks: int = 2


def slope(diff):
    return diff * lax.rsqrt(diff * diff + 0.01)


def kernel(sz, mesh_r, grid_r, edges_r, truth_r, area_r, cw_r, gain_r, wh_r, wo_r,
           gh_o, go_o, gg_o, pg_o,
           wbuf, halo, normed, norm_t, act_t, pre, gprime, pred_s, truth_s, cw_s,
           pall, pair_s, pair_r, gb, dp_send, dp_half, dout_s,
           mb, r1, s1, s2, r2, s3f, s3, r3, ob, obf, o1, o2, o2s, o2f, r4, fin_s, fin, fo_s, fo,
           wz_s, wz_r, wy_s, wy_r, wc_s, wc_r, ha_s, ha_r, tc_s, tc_r, p1_s, p1_r, p2_s, p2_r,
           p4_s, p4_r, q1_s, q1_r, q2_s, q2_r, q3_s, q3_r, q4_s, q4_r, q5_s, q5_r, q6_s, q6_r,
           u1_s, u1_r, u2_s, u2_r):
    nx, ny, nzl, nzh = sz.x, sz.y, sz.zl, sz.zh
    nz = nzl * nzh
    hid = nzl * ny * 2 * ROWS
    slab = ny * 2 * ROWS
    half = hid // 2
    tile = half // nx
    pts, pad, nch = sz.points, sz.pad, sz.chunks
    quarter = pad // nzh
    two = 2 * ROWS
    zpc = nzl // nch

    ens, grd = lax.axis_index("ens"), lax.axis_index("grid")
    x, zh = lax.div(ens, nzh), lax.rem(ens, nzh)
    c = lax.rem(grd, 2)
    y = lax.rem(lax.div(grd, 2), ny)
    zl = lax.div(grd, 2 * ny)
    z = zh * nzl + zl
    oc = 1 - c
    ngrid = nzl * ny * 2

    def at(x_, y_, z_, c_):
        return (x_ * nzh + lax.div(z_, nzl), (lax.rem(z_, nzl) * ny + y_) * 2 + c_)

    window = []
    for d in range(1, nzl // 2 + 1):
        window.append(d)
        if d < nzl // 2 or nzl == 1:
            window.append(-d)
    window = window[: nzl - 1]

    def zdev(d):
        return at(x, y, lax.rem(z + d + nz, nz), c)

    def zhdev(i):
        return at(x, y, lax.rem(zh + i, nzh) * nzl + zl, c)

    def ydev(i):
        return at(x, lax.rem(y + i, ny), z, c)

    def xdev(i, c_):
        return at(lax.rem(x + i, nx), y, z, c_)

    left = (ens, lax.rem(grd + ngrid - 1, ngrid))
    right = (ens, lax.rem(grd + 1, ngrid))
    other = at(x, y, z, oc)

    partners = [zdev(d) for d in window] + [zdev(-d) for d in window]
    partners += [zhdev(i) for i in range(1, nzh)]
    partners += [ydev(i) for i in range(1, ny)]
    partners += [xdev(i, c) for i in range(1, nx)] + [xdev(i, oc) for i in range(1, nx)]
    partners += [left, right, other]
    barrier = pltpu.get_barrier_semaphore()
    for dev in partners:
        pl.semaphore_signal(barrier, inc=1, device_id=dev, device_id_type=pl.DeviceIdType.MESH)

    sent = []

    def copy(src, dst, ssem, rsem, dev):
        return pltpu.make_async_remote_copy(
            src_ref=src, dst_ref=dst, send_sem=ssem, recv_sem=rsem,
            device_id=dev, device_id_type=pl.DeviceIdType.MESH)

    def go(cp):
        cp.start()
        sent.append(cp)
        return cp

    wbuf[zl, y, c, :, pl.ds(0, hid)] = wh_r[...]
    wbuf[zl, y, c, :, pl.ds(hid, pad)] = jnp.zeros((ROWS, pad), BF16)
    wbuf[zl, y, c, :, pl.ds(hid, sz.chans)] = wo_r[...]
    pl.semaphore_wait(barrier, len(partners))

    offs = [0] + window
    wz = []
    for s in range(1, nzl):
        blk = wbuf.at[zl, y, c]
        wz.append(go(copy(blk, blk, wz_s.at[s], wz_r.at[s], zdev(offs[s]))))
    ha = [go(copy(mesh_r, halo.at[0], ha_s.at[0], ha_r.at[0], right)),
          go(copy(mesh_r, halo.at[1], ha_s.at[1], ha_r.at[1], left))]

    def zof(s):
        return lax.rem(zl - offs[s] + nzl, nzl)

    def wy_start(s):
        blk = wbuf.at[zof(s), y, c]
        return [go(copy(blk, blk, wy_s.at[s, i - 1], wy_r.at[s, i - 1], ydev(i)))
                for i in range(1, ny)]

    def wc_start(s):
        blk = wbuf.at[zof(s), :, c]
        return go(copy(blk, blk, wc_s.at[s], wc_r.at[s], other))

    wy, wc = {}, {}
    wy[0] = wy_start(0)

    local = (edges_r[...] - (grd - 1) * sz.nodes + ngrid * sz.nodes) % (ngrid * sz.nodes)
    lane = lax.broadcasted_iota(jnp.int32, (pts, sz.nodes), 1)

    def counts(base):
        total = jnp.zeros((pts, sz.nodes), F32)
        for k in range(3):
            total += jnp.where(local[:, k:k + 1] == lane + base, 1.0, 0.0)
        return total.astype(BF16)

    agg = jnp.dot(counts(sz.nodes), mesh_r[...], preferred_element_type=F32)
    ha[0].wait_recv()
    agg += jnp.dot(counts(0), halo[0], preferred_element_type=F32)
    ha[1].wait_recv()
    agg += jnp.dot(counts(2 * sz.nodes), halo[1], preferred_element_type=F32)
    state = grid_r[...].astype(F32) + agg / 3.0
    center = state - jnp.mean(state, axis=-1, keepdims=True)
    var = jnp.mean(center * center, axis=-1, keepdims=True)
    pre[...] = center * lax.rsqrt(var + LN_EPS) * gain_r[...]
    normed[...] = pre[...].astype(BF16)

    def turn(src, dst):
        def step(k, carry):
            cols = pl.ds(pl.multiple_of(k * slab, slab), slab)
            dst[c, cols, :] = src[:, cols].T.astype(BF16)
            return carry
        lax.fori_loop(0, nzl, step, 0)

    turn(pre, norm_t)
    tn = go(copy(norm_t.at[c], norm_t.at[c], tc_s.at[0], tc_r.at[0], other))
    pre[...] = jnp.zeros((pts, hid), F32)

    for s in range(1, nzl + 3):
        if s < nzl:
            wz[s - 1].wait_recv()
            wy[s] = wy_start(s)
        t = s - 2
        if 0 <= t < nzl:
            for cp in wy[t]:
                cp.wait_recv()
            wc[t] = wc_start(t)
        u = s - 3
        if 0 <= u < nzl:
            wc[u].wait_recv()
            zu = zof(u)
            cols = pl.ds(pl.multiple_of(zu * slab, slab), slab)
            pre[...] += jnp.dot(
                normed[:, cols], wbuf[zu, :, :, :, pl.ds(0, hid)].reshape(slab, hid),
                preferred_element_type=F32)

    k0, k1 = 0.7978845608028654, 0.044715
    v = pre[...]
    act = 0.5 * v * (1.0 + jnp.tanh(k0 * (v + k1 * v * v * v)))
    wout = wbuf[:, :, :, :, pl.ds(hid, pad)].reshape(hid, pad)
    pred_t = jnp.dot(act.astype(BF16), wout, preferred_element_type=F32)
    pred_s[...] = pred_t.T.astype(BF16).reshape(nzh, quarter, pts)
    p1 = []
    for i in range(1, nzh):
        to = lax.rem(zh + i, nzh)
        p1.append(go(copy(pred_s.at[to], pall.at[x, zh], p1_s.at[i - 1], p1_r.at[i - 1], zhdev(i))))
    pall[x, zh] = pred_s[zh]
    th = jnp.tanh(k0 * (v + k1 * v * v * v))
    gprime[...] = 0.5 * (1.0 + th) + 0.5 * v * (1.0 - th * th) * (k0 * (1.0 + 3.0 * k1 * v * v))
    pre[...] = 0.5 * v * (1.0 + th)
    turn(pre, act_t)
    ta = go(copy(act_t.at[c], act_t.at[c], tc_s.at[1], tc_r.at[1], other))
    truth_s[...] = jnp.zeros_like(truth_s)
    truth_s[pl.ds(0, sz.chans), :] = truth_r[...]
    cw_s[...] = jnp.zeros_like(cw_s)
    cw_s[pl.ds(0, 1), pl.ds(0, sz.chans)] = cw_r[...]
    weight = jnp.broadcast_to(cw_s[pl.ds(0, 1), :], (pad, pad)).T[:, 0:1] * area_r[...]
    own = pred_s[...].reshape(pad, pts).astype(F32)
    own = slope(own - truth_s[...])
    for cp in p1:
        cp.wait_recv()
    p2 = []
    for i in range(1, nx):
        p2.append(go(copy(pall.at[x], pall.at[x], p2_s.at[i - 1], p2_r.at[i - 1], xdev(i, c))))
    mine = pall[x].astype(F32)
    pair = jnp.zeros((nzh, quarter, pts), F32)
    for i in range(nx):
        if i > 0:
            p2[i - 1].wait_recv()
        src = lax.rem(x - i + nx, nx)
        for j in range(nzh):
            pair += slope(mine - pall[src, j].astype(F32)[None])
    pair_s[...] = pair.astype(BF16)
    p4 = []
    for i in range(1, nzh):
        to = lax.rem(zh + i, nzh)
        p4.append(go(copy(pair_s.at[to], pair_r.at[zh], p4_s.at[i - 1], p4_r.at[i - 1], zhdev(i))))
    pair_r[zh] = pair_s[zh]
    for cp in p4:
        cp.wait_recv()
    pgrad = weight * (own - pair_r[...].astype(F32).reshape(pad, pts) / (nx * nzh - 1.0))
    pg_o[...] = pgrad[0:sz.chans, :]
    gb[c] = pgrad.T.astype(BF16)
    tg = go(copy(gb.at[c], gb.at[c], tc_s.at[2], tc_r.at[2], other))

    def d_pre(which):
        zz = pl.ds(which * (nzl // 2), nzl // 2)
        w = wbuf[zz, :, :, :, pl.ds(hid, pad)].reshape(half, pad)
        d_act = lax.dot_general(gb[c], w, NT, preferred_element_type=F32)
        return (d_act * gprime[:, pl.ds(pl.multiple_of(which * half, half), half)]).astype(BF16)

    dp_send[...] = d_pre(oc)
    td = go(copy(dp_send, dp_half.at[c], tc_s.at[3], tc_r.at[3], other))
    dp_half[c] = d_pre(c)
    tn.wait_recv()
    td.wait_recv()

    me_a, me_b = x + (y - x) * c, y + (x - y) * c
    na = nx
    def adev(i):
        to = lax.rem(me_a + i, na)
        return to, at(to + (x - to) * c, y + (to - y) * c, z, c)

    def bdev(i):
        to = lax.rem(me_b + i, na)
        return to, at(x + (to - x) * c, to + (y - to) * c, z, c)

    q1, q2 = {}, {}
    for ch in range(nch):
        def step(k, carry):
            rows = pl.ds(pl.multiple_of((ch * zpc + k) * slab, slab), slab)
            lhs = jnp.concatenate([norm_t[0, rows, :], norm_t[1, rows, :]], axis=1)
            res = jnp.dot(lhs, dp_half[...].reshape(2 * pts, half), preferred_element_type=F32)
            res = res.astype(BF16)
            for yy in range(ny):
                for xx in range(nx):
                    a, b = xx + (yy - xx) * c, yy + (xx - yy) * c
                    mb[ch, a, b, pl.ds(pl.multiple_of(k * two, two), two), :] = (
                        res[yy * two:(yy + 1) * two, xx * tile:(xx + 1) * tile])
            return carry
        lax.fori_loop(0, zpc, step, 0)
        for i in range(1, na):
            to, dev = adev(i)
            q1[ch, i] = go(copy(mb.at[ch, to], r1.at[ch, i - 1], q1_s.at[ch, i - 1],
                                q1_r.at[ch, i - 1], dev))

    ta.wait_recv()
    tg.wait_recv()

    def out_step(k, carry):
        rows = pl.ds(pl.multiple_of(k * slab, slab), slab)
        lhs = jnp.concatenate([act_t[0, rows, :], act_t[1, rows, :]], axis=1)
        res = jnp.dot(lhs, gb[...].reshape(2 * pts, pad), preferred_element_type=F32)
        dout_s[...] = res.reshape(ny, 2, ROWS, pad)
        part = dout_s[:, c]
        obf[k] = part
        ob[k] = part.astype(BF16)
        return carry

    lax.fori_loop(0, nzl, out_step, 0)
    u1 = []
    for j, d in enumerate(window):
        to = lax.rem(zl + d + nzl, nzl)
        u1.append(go(copy(ob.at[to], o1.at[j], u1_s.at[j], u1_r.at[j], zdev(d))))

    for ch in range(nch):
        for i in range(1, na):
            q1[ch, i].wait_recv()
        total = mb[ch, me_a].astype(F32)
        for i in range(1, na):
            total += r1[ch, i - 1].astype(F32)
        s1[ch] = total
        s2[ch] = total.astype(BF16)
        for i in range(1, na):
            to, dev = bdev(i)
            q2[ch, i] = go(copy(s2.at[ch, to], r2.at[ch, i - 1], q2_s.at[ch, i - 1],
                                q2_r.at[ch, i - 1], dev))
    for cp in u1:
        cp.wait_recv()
    total = obf[zl]
    for j in range(len(window)):
        total += o1[j].astype(F32)
    o2f[...] = total
    o2s[...] = total.astype(BF16)
    u2 = []
    for i in range(1, ny):
        to = lax.rem(y + i, ny)
        u2.append(go(copy(o2s.at[to], o2.at[i - 1], u2_s.at[i - 1], u2_r.at[i - 1], ydev(i))))
    for ch in range(nch):
        for i in range(1, na):
            q2[ch, i].wait_recv()
        total = s1[ch, me_b]
        for i in range(1, na):
            total += r2[ch, i - 1].astype(F32)
        s3f[pl.ds(ch * zpc, zpc)] = total.reshape(zpc, two, tile)
        s3[pl.ds(ch * zpc, zpc)] = total.reshape(zpc, two, tile).astype(BF16)
    q3 = []
    for j, d in enumerate(window):
        to = lax.rem(zl + d + nzl, nzl)
        q3.append(go(copy(s3.at[to], r3.at[j], q3_s.at[j], q3_r.at[j], zdev(d))))
    for cp in u2:
        cp.wait_recv()
    ototal = o2f[y]
    for i in range(1, ny):
        ototal += o2[i - 1].astype(F32)
    r4[zh, pl.ds(two, ROWS), :] = ototal.astype(BF16)
    for cp in q3:
        cp.wait_recv()
    total = s3f[zl]
    for j in range(len(window)):
        total += r3[j].astype(F32)
    r4[zh, pl.ds(0, two), :] = total.astype(BF16)
    q4 = []
    for i in range(1, nzh):
        q4.append(go(copy(r4.at[zh], r4.at[zh], q4_s.at[i - 1], q4_r.at[i - 1], zhdev(i))))
    for cp in q4:
        cp.wait_recv()
    total = r4[0].astype(F32)
    for i in range(1, nzh):
        total += r4[i].astype(F32)
    fin_s[...] = total[0:two].reshape(2, ROWS, tile)
    fo[x] = total[two:two + ROWS]
    mine_t = c * nx + x
    fin[mine_t] = fin_s[c]
    q5, q6 = [], []
    q5.append(go(copy(fin_s.at[oc], fin.at[mine_t], q5_s.at[0], q5_r.at[0], other)))
    for i in range(1, nx):
        q5.append(go(copy(fin_s.at[c], fin.at[mine_t], q5_s.at[i], q5_r.at[i], xdev(i, c))))
        q5.append(go(copy(fin_s.at[oc], fin.at[mine_t], q5_s.at[nx + i - 1], q5_r.at[nx + i - 1],
                          xdev(i, oc))))
        q6.append(go(copy(fo.at[x], fo.at[x], q6_s.at[i - 1], q6_r.at[i - 1], xdev(i, c))))
    for cp in q6:
        cp.wait_recv()
    for cp in q5:
        cp.wait_recv()

    scale = 1.0 / math.sqrt(nx * nzh * pts * ngrid)
    total = fo[0]
    for i in range(1, nx):
        total += fo[i]
    go_o[...] = (total * scale)[:, 0:sz.chans]
    dots = jnp.zeros((ROWS, 1), F32)
    for t in range(2 * nx):
        part = fin[t] * scale
        gh_o[:, pl.ds(t * tile, tile)] = part
        dots += jnp.sum(part * wh_r[:, pl.ds(t * tile, tile)].astype(F32), axis=-1, keepdims=True)
    row = lax.broadcasted_iota(jnp.int32, (ROWS, hid), 0)
    col = lax.broadcasted_iota(jnp.int32, (ROWS, hid), 1)
    gains = jnp.sum(jnp.where(col == row + grd * ROWS, gain_r[...], 0.0), axis=-1, keepdims=True)
    dots = dots / gains
    row = lax.broadcasted_iota(jnp.int32, (ROWS, ROWS), 0)
    col = lax.broadcasted_iota(jnp.int32, (ROWS, ROWS), 1)
    gg_o[...] = jnp.sum(jnp.where(row == col, dots, 0.0), axis=0, keepdims=True)

    for cp in sent:
        cp.wait_send()


def body(sz, mesh_latent, grid_latent, edges, truth, area, chan_weight, gain, w_hidden, w_out):
    nx, ny, nzl, nzh = sz.x, sz.y, sz.zl, sz.zh
    hid = nzl * ny * 2 * ROWS
    half = hid // 2
    tile = half // nx
    pts, pad, nch = sz.points, sz.pad, sz.chunks
    quarter = pad // nzh
    zpc = nzl // nch
    rc = zpc * 2 * ROWS
    win = max(nzl - 1, 1)
    V = pltpu.VMEM

    def sems(*shape):
        return [pltpu.SemaphoreType.DMA(shape)] * 2

    scratch = [
        V((nzl, ny, 2, ROWS, hid + pad), BF16),
        V((2, sz.nodes, hid), BF16),
        V((pts, hid), BF16),
        V((2, hid, pts), BF16),
        V((2, hid, pts), BF16),
        V((pts, hid), F32),
        V((pts, hid), F32),
        V((nzh, quarter, pts), BF16),
        V((pad, pts), F32),
        V((8, pad), F32),
        V((nx, nzh, quarter, pts), BF16),
        V((nzh, quarter, pts), BF16),
        V((nzh, quarter, pts), BF16),
        V((2, pts, pad), BF16),
        V((pts, half), BF16),
        V((2, pts, half), BF16),
        V((ny, 2, ROWS, pad), F32),
        V((nch, nx, ny, rc, tile), BF16),
        V((nch, nx - 1, ny, rc, tile), BF16),
        V((nch, ny, rc, tile), F32),
        V((nch, ny, rc, tile), BF16),
        V((nch, ny - 1, rc, tile), BF16),
        V((nzl, 2 * ROWS, tile), F32),
        V((nzl, 2 * ROWS, tile), BF16),
        V((win, 2 * ROWS, tile), BF16),
        V((nzl, ny, ROWS, pad), BF16),
        V((nzl, ny, ROWS, pad), F32),
        V((win, ny, ROWS, pad), BF16),
        V((ny - 1, ROWS, pad), BF16),
        V((ny, ROWS, pad), BF16),
        V((ny, ROWS, pad), F32),
        V((nzh, 3 * ROWS, tile), BF16),
        V((2, ROWS, tile), F32),
        V((2 * nx, ROWS, tile), F32),
        V((8, 128), F32),
        V((nx, ROWS, pad), F32),
    ]
    scratch += sems(nzl) + sems(nzl, ny - 1) + sems(nzl) + sems(2) + sems(4)
    scratch += sems(nzh - 1) + sems(nx - 1) + sems(nzh - 1)
    scratch += sems(nch, nx - 1) + sems(nch, ny - 1) + sems(win) + sems(nzh - 1)
    scratch += sems(2 * nx - 1) + sems(nx - 1) + sems(win) + sems(ny - 1)
    vmem = pl.BlockSpec(memory_space=pltpu.VMEM)
    outs = pl.pallas_call(
        functools.partial(kernel, sz),
        out_shape=(
            jax.ShapeDtypeStruct((ROWS, hid), F32),
            jax.ShapeDtypeStruct((ROWS, sz.chans), F32),
            jax.ShapeDtypeStruct((1, ROWS), F32),
            jax.ShapeDtypeStruct((sz.chans, pts), F32),
        ),
        in_specs=[vmem] * 9,
        out_specs=(vmem,) * 4,
        scratch_shapes=scratch,
        compiler_params=pltpu.CompilerParams(
            collective_id=0, has_side_effects=True, vmem_limit_bytes=40 * 1024 * 1024),
        cost_estimate=pl.CostEstimate(flops=10**9, bytes_accessed=10**6, transcendentals=10**6),
    )(mesh_latent[0], grid_latent[0], edges, truth, area[None], chan_weight[None], gain[None],
      w_hidden, w_out)
    return outs[0], outs[1], outs[2][0], outs[3][None]


def program(mesh, sz):
    return jax.shard_map(
        functools.partial(body, sz),
        mesh=mesh,
        in_specs=(
            P("ens", "grid", None),
            P("ens", "grid", None),
            P("grid", None),
            P(None, "grid"),
            P("grid"),
            P(),
            P(),
            P("grid", None),
            P("grid", None),
        ),
        out_specs=(P("grid", None), P("grid", None), P("grid"), P("ens", None, "grid")),
        check_vma=False,
    )


def solution(mesh):
    return program(mesh, Sizes())
```

```python
import functools
import math
from typing import NamedTuple

import jax
import jax.numpy as jnp
from jax import lax
from jax.experimental import pallas as pl
from jax.experimental.pallas import tpu as pltpu
from jax.sharding import PartitionSpec as P

LN_EPS = 1e-05
F32, BF16 = jnp.float32, jnp.bfloat16
ROWS = 16
NT = (((1,), (1,)), ((), ()))


class Sizes(NamedTuple):
    x: int = 4
    y: int = 4
    zl: int = 8
    zh: int = 4
    points: int = 128
    nodes: int = 64
    chans: int = 100
    pad: int = 128
    chunks: int = 4


def slope(diff):
    return diff * lax.rsqrt(diff * diff + 0.01)


def kernel(sz, mesh_h, grid_h, edges_h, truth_h, area_h, cw_h, gain_h, wh_h, wo_h,
           gh_o, go_o, gg_o, pg_o,
           mesh_r, grid_r, edges_r, truth_r, area_r, cw_r, gain_r, wo_r,
           wbuf, halo, normed, norm_t, act_t, pre, gprime, pred_s, truth_s, cw_s,
           pall, pair_s, pair_r, gb, dp_send, dp_half, dout_s,
           mb, r1, s1, s2, r2, s3, r3, ob, obf, o1, o2, o2s, o2f, r4, fin_s, fin, fo,
           near, far, lo_s,
           wz_s, wz_r, wy_s, wy_r, wx_s, wx_r, wc_s, wc_r, ha_s, ha_r, tc_s, tc_r,
           p1_s, p1_r, p2_s, p2_r,
           p4_s, p4_r, q1_s, q1_r, q2_s, q2_r, q3_s, q3_r, q4_s, q4_r, q5_s, q5_r, q6_s, q6_r,
           u1_s, u1_r, u2_s, u2_r):
    nx, ny, nzl, nzh = sz.x, sz.y, sz.zl, sz.zh
    nz = nzl * nzh
    hid = nzl * ny * 2 * ROWS
    slab = ny * 2 * ROWS
    half = hid // 2
    tile = half // nx
    pts, pad, nch = sz.points, sz.pad, sz.chunks
    quarter = pad // nx
    two = 2 * ROWS
    zpc = nzl // nch

    ens, grd = lax.axis_index("ens"), lax.axis_index("grid")
    x, zh = lax.div(ens, nzh), lax.rem(ens, nzh)
    c = lax.rem(grd, 2)
    y = lax.rem(lax.div(grd, 2), ny)
    zl = lax.div(grd, 2 * ny)
    z = zh * nzl + zl
    oc = 1 - c
    ngrid = nzl * ny * 2

    def at(x_, y_, z_, c_):
        return (x_ * nzh + lax.div(z_, nzl), (lax.rem(z_, nzl) * ny + y_) * 2 + c_)

    window = []
    for d in range(1, nzl // 2 + 1):
        window.append(d)
        if d < nzl // 2 or nzl == 1:
            window.append(-d)
    window = window[: nzl - 1]

    def zdev(d):
        return at(x, y, lax.rem(z + d + nz, nz), c)

    def zhdev(i):
        return at(x, y, lax.rem(zh + i, nzh) * nzl + zl, c)

    def ydev(i):
        return at(x, lax.rem(y + i, ny), z, c)

    def xdev(i, c_):
        return at(lax.rem(x + i, nx), y, z, c_)

    left = (ens, lax.rem(grd + ngrid - 1, ngrid))
    right = (ens, lax.rem(grd + 1, ngrid))
    other = at(x, y, z, oc)

    def signal(sem, dev):
        pl.semaphore_signal(sem, inc=1, device_id=dev, device_id_type=pl.DeviceIdType.MESH)

    partners = [zdev(d) for d in window] + [zdev(-d) for d in window]
    partners += [ydev(i) for i in range(1, ny)]
    partners += [xdev(i, c) for i in range(1, nx)] + [xdev(i, oc) for i in range(1, nx)]
    partners += [left, right, other]
    barrier = pltpu.get_barrier_semaphore()
    for dev in partners:
        signal(barrier, dev)

    def fetch(k, src, dst):
        cp = pltpu.make_async_copy(src, dst, lo_s.at[k])
        cp.start()
        return cp

    lo_m = [fetch(2, mesh_h, mesh_r), fetch(3, edges_h, edges_r), fetch(4, grid_h, grid_r),
            fetch(5, gain_h, gain_r)]
    lo_t = [fetch(6, truth_h, truth_r), fetch(7, area_h, area_r), fetch(8, cw_h, cw_r)]

    sent = []

    def copy(src, dst, ssem, rsem, dev):
        return pltpu.make_async_remote_copy(
            src_ref=src, dst_ref=dst, send_sem=ssem, recv_sem=rsem,
            device_id=dev, device_id_type=pl.DeviceIdType.MESH)

    def go(cp):
        cp.start()
        sent.append(cp)
        return cp

    odd = lax.rem(zl, 2)
    zb = 2 * x + 1
    spread = jnp.logical_or(odd == 0, zl == zb)

    @pl.when(spread)
    def _():
        wbuf[zl, y, c, :, pl.ds(hid, pad)] = jnp.zeros((ROWS, pad), BF16)
        lo_w = [fetch(0, wh_h, wbuf.at[zl, y, c, :, pl.ds(0, hid)]), fetch(1, wo_h, wo_r)]
        for cp in lo_w:
            cp.wait()
        wbuf[zl, y, c, :, pl.ds(hid, sz.chans)] = wo_r[...]

    pl.semaphore_wait(barrier, len(partners))

    reach = nzl // 2
    signal(near, zdev(reach))
    signal(near, zdev(-reach))

    block = wbuf.at[zl, y, c]
    wz = {d: copy(block, block, wz_s.at[j], wz_r.at[zl], zdev(d)) for j, d in enumerate(window)}

    @pl.when(spread)
    def _():
        for d in window:
            wz[d].start()

    def wz_wait(zk):
        got = wbuf.at[zk, y, c]
        copy(got, got, wz_s.at[0], wz_r.at[zk], zdev(1)).wait_recv()

    def wy_start(zk):
        blk = wbuf.at[zk, y, c]
        return [go(copy(blk, blk, wy_s.at[zk, i - 1], wy_r.at[zk, i - 1], ydev(i)))
                for i in range(1, ny)]

    def wc_start(zk):
        blk = wbuf.at[zk, :, c]
        return go(copy(blk, blk, wc_s.at[zk], wc_r.at[zk], other))

    evens = [0] + [-d for d in window if d % 2 == 0]
    odds = [-d for d in window if d % 2 == 1]
    za = [lax.rem(zl + e + (o - e) * odd + nzl, nzl) for e, o in zip(evens, odds, strict=True)]
    nk = len(za)
    wy = {}

    @pl.when(odd == 1)
    def _():
        wz_wait(za[0])
    wy[0] = wy_start(za[0])
    ha = [go(copy(mesh_h, halo.at[0], ha_s.at[0], ha_r.at[0], right)),
          go(copy(mesh_h, halo.at[1], ha_s.at[1], ha_r.at[1], left))]

    for cp in lo_m:
        cp.wait()
    local = (edges_r[...] - (grd - 1) * sz.nodes + ngrid * sz.nodes) % (ngrid * sz.nodes)
    node = lax.broadcasted_iota(jnp.int32, (sz.nodes, pts), 0)

    def counts(base):
        total = jnp.zeros((sz.nodes, pts), F32)
        for k in range(3):
            total += jnp.where(local[k:k + 1, :] == node + base, 1.0, 0.0)
        return total.T.astype(BF16)

    agg = jnp.dot(counts(sz.nodes), mesh_r[...], preferred_element_type=F32)
    for k in range(1, nk - 1):
        wz_wait(za[k])
        wy[k] = wy_start(za[k])
    ha[0].wait_recv()
    agg += jnp.dot(counts(0), halo[0], preferred_element_type=F32)
    ha[1].wait_recv()
    agg += jnp.dot(counts(2 * sz.nodes), halo[1], preferred_element_type=F32)
    state = grid_r[...].astype(F32) + agg / 3.0
    center = state - jnp.mean(state, axis=-1, keepdims=True)
    var = jnp.mean(center * center, axis=-1, keepdims=True)
    pre[...] = center * lax.rsqrt(var + LN_EPS) * gain_r[...]
    normed[...] = pre[...].astype(BF16)

    def turn(src, dst):
        def step(k, carry):
            cols = pl.ds(pl.multiple_of(k * slab, slab), slab)
            dst[c, cols, :] = src[:, cols].T.astype(BF16)
            return carry
        lax.fori_loop(0, nzl, step, 0)

    turn(pre, norm_t)
    tn = go(copy(norm_t.at[c], norm_t.at[c], tc_s.at[0], tc_r.at[0], other))
    pre[...] = jnp.zeros((pts, hid), F32)

    @pl.when(zl != zb)
    def _():
        wz_wait(zb)
    wyb = wy_start(zb)
    if nk > 1:
        wz_wait(za[nk - 1])
        wy[nk - 1] = wy_start(za[nk - 1])

    def slab_in(k):
        for cp in wy[k]:
            cp.wait_recv()
        wc_start(za[k])

    def multiply(zk):
        got = wbuf.at[zk, :, oc]
        copy(got, got, wc_s.at[zk], wc_r.at[zk], other).wait_recv()
        cols = pl.ds(pl.multiple_of(zk * slab, slab), slab)
        pre[...] += jnp.dot(
            normed[:, cols], wbuf[zk, :, :, :, pl.ds(0, hid)].reshape(slab, hid),
            preferred_element_type=F32)

    slab_in(0)
    for cp in wyb:
        cp.wait_recv()
    wx = []
    for i in range(1, nx):
        blk = wbuf.at[zb, :, c]
        wx.append(go(copy(blk, blk, wx_s.at[i - 1], wx_r.at[i - 1], xdev(i, c))))
    wc_start(zb)
    pl.semaphore_wait(near, 2)
    signal(far, zhdev(1))
    signal(far, zhdev(nzh - 1))
    for k in range(1, nk):
        slab_in(k)
        multiply(za[k - 1])
    multiply(zb)
    zx = [2 * lax.rem(x - i + nx, nx) + 1 for i in range(nx)]
    order = [1] + ([nx - 1] if nx > 2 else []) + list(range(2, nx - 1))
    for k, i in enumerate(order):
        got = wbuf.at[zx[i], :, c]
        copy(got, got, wx_s.at[i - 1], wx_r.at[i - 1], xdev(i, c)).wait_recv()
        wc_start(zx[i])
        multiply(za[nk - 1] if k == 0 else zx[order[k - 1]])
    multiply(zx[order[-1]])

    k0, k1 = 0.7978845608028654, 0.044715
    v = pre[...]
    act = 0.5 * v * (1.0 + jnp.tanh(k0 * (v + k1 * v * v * v)))
    wout = wbuf[:, :, :, :, pl.ds(hid, pad)].reshape(hid, pad)
    pred_t = jnp.dot(act.astype(BF16), wout, preferred_element_type=F32)
    pred_s[...] = pred_t.T.astype(BF16).reshape(nx, quarter, pts)
    p1 = []
    for i in range(1, nx):
        to = lax.rem(x + i, nx)
        p1.append(go(copy(pred_s.at[to], pall.at[zh, x], p1_s.at[i - 1], p1_r.at[i - 1], xdev(i, c))))
    pall[zh, x] = pred_s[x]
    pl.semaphore_wait(far, 2)
    for cp in p1:
        cp.wait_recv()
    zorder = [nzh // 2] + [i for i in range(1, nzh) if i != nzh // 2]
    p2 = {}
    for i in zorder:
        p2[i] = go(copy(pall.at[zh], pall.at[zh], p2_s.at[i - 1], p2_r.at[i - 1], zhdev(i)))
    th = jnp.tanh(k0 * (v + k1 * v * v * v))
    gprime[...] = 0.5 * (1.0 + th) + 0.5 * v * (1.0 - th * th) * (k0 * (1.0 + 3.0 * k1 * v * v))
    pre[...] = 0.5 * v * (1.0 + th)
    turn(pre, act_t)
    ta = go(copy(act_t.at[c], act_t.at[c], tc_s.at[1], tc_r.at[1], other))
    for cp in lo_t:
        cp.wait()
    truth_s[...] = jnp.zeros_like(truth_s)
    truth_s[pl.ds(0, sz.chans), :] = truth_r[...]
    cw_s[...] = jnp.zeros_like(cw_s)
    cw_s[pl.ds(0, 1), pl.ds(0, sz.chans)] = cw_r[...]
    weight = jnp.broadcast_to(cw_s[pl.ds(0, 1), :], (pad, pad)).T[:, 0:1] * area_r[...]
    own = pred_s[...].reshape(pad, pts).astype(F32)
    own = slope(own - truth_s[...])
    mine = pall[zh].astype(F32)
    pair = jnp.zeros((nx, quarter, pts), F32)
    for i in [0] + zorder[1:] + zorder[:1]:
        if i > 0:
            p2[i].wait_recv()
        src = lax.rem(zh - i + nzh, nzh)
        for j in range(nx):
            pair += slope(mine - pall[src, j].astype(F32)[None])
    pair_s[...] = pair.astype(BF16)
    p4 = []
    for i in range(1, nx):
        to = lax.rem(x + i, nx)
        p4.append(go(copy(pair_s.at[to], pair_r.at[x], p4_s.at[i - 1], p4_r.at[i - 1], xdev(i, c))))
    pair_r[x] = pair_s[x]
    for cp in p4:
        cp.wait_recv()
    pgrad = weight * (own - pair_r[...].astype(F32).reshape(pad, pts) / (nx * nzh - 1.0))
    pg_o[...] = pgrad[0:sz.chans, :]
    gb[c] = pgrad.T.astype(BF16)
    tg = go(copy(gb.at[c], gb.at[c], tc_s.at[2], tc_r.at[2], other))

    def d_pre(which):
        zz = pl.ds(which * (nzl // 2), nzl // 2)
        w = wbuf[zz, :, :, :, pl.ds(hid, pad)].reshape(half, pad)
        d_act = lax.dot_general(gb[c], w, NT, preferred_element_type=F32)
        return (d_act * gprime[:, pl.ds(pl.multiple_of(which * half, half), half)]).astype(BF16)

    dp_send[...] = d_pre(oc)
    td = go(copy(dp_send, dp_half.at[c], tc_s.at[3], tc_r.at[3], other))
    dp_half[c] = d_pre(c)
    tn.wait_recv()
    td.wait_recv()

    me_a, me_b = x + (y - x) * c, y + (x - y) * c
    na = nx
    def adev(i):
        to = lax.rem(me_a + i, na)
        return to, at(to + (x - to) * c, y + (to - y) * c, z, c)

    def bdev(i):
        to = lax.rem(me_b + i, na)
        return to, at(x + (to - x) * c, to + (y - to) * c, z, c)

    q1, q2 = {}, {}
    for ch in range(nch):
        def step(k, carry):
            rows = pl.ds(pl.multiple_of((ch * zpc + k) * slab, slab), slab)
            lhs = jnp.concatenate([norm_t[0, rows, :], norm_t[1, rows, :]], axis=1)
            res = jnp.dot(lhs, dp_half[...].reshape(2 * pts, half), preferred_element_type=F32)
            res = res.astype(BF16)
            for yy in range(ny):
                for xx in range(nx):
                    a, b = xx + (yy - xx) * c, yy + (xx - yy) * c
                    mb[ch, a, b, pl.ds(pl.multiple_of(k * two, two), two), :] = (
                        res[yy * two:(yy + 1) * two, xx * tile:(xx + 1) * tile])
            return carry
        lax.fori_loop(0, zpc, step, 0)
        for i in range(1, na):
            to, dev = adev(i)
            q1[ch, i] = go(copy(mb.at[ch, to], r1.at[ch, i - 1], q1_s.at[ch, i - 1],
                                q1_r.at[ch, i - 1], dev))

    ta.wait_recv()
    tg.wait_recv()

    def out_step(k, carry):
        rows = pl.ds(pl.multiple_of(k * slab, slab), slab)
        lhs = jnp.concatenate([act_t[0, rows, :], act_t[1, rows, :]], axis=1)
        res = jnp.dot(lhs, gb[...].reshape(2 * pts, pad), preferred_element_type=F32)
        dout_s[...] = res.reshape(ny, 2, ROWS, pad)
        part = dout_s[:, c]
        obf[k] = part
        ob[k] = part.astype(BF16)
        return carry

    lax.fori_loop(0, nzl, out_step, 0)
    u1 = []
    for j, d in enumerate(window):
        to = lax.rem(zl + d + nzl, nzl)
        u1.append(go(copy(ob.at[to], o1.at[j], u1_s.at[j], u1_r.at[j], zdev(d))))

    for ch in range(nch):
        for i in range(1, na):
            q1[ch, i].wait_recv()
        total = mb[ch, me_a].astype(F32)
        for i in range(1, na):
            total += r1[ch, i - 1].astype(F32)
        s1[ch] = total
        s2[ch] = total.astype(BF16)
        for i in range(1, na):
            to, dev = bdev(i)
            q2[ch, i] = go(copy(s2.at[ch, to], r2.at[ch, i - 1], q2_s.at[ch, i - 1],
                                q2_r.at[ch, i - 1], dev))
    for cp in u1:
        cp.wait_recv()
    total = obf[zl]
    for j in range(len(window)):
        total += o1[j].astype(F32)
    o2f[...] = total
    o2s[...] = total.astype(BF16)
    u2 = []
    for i in range(1, ny):
        to = lax.rem(y + i, ny)
        u2.append(go(copy(o2s.at[to], o2.at[i - 1], u2_s.at[i - 1], u2_r.at[i - 1], ydev(i))))
    q3 = {}
    for ch in range(nch):
        for i in range(1, na):
            q2[ch, i].wait_recv()
        total = s1[ch, me_b]
        for i in range(1, na):
            total += r2[ch, i - 1].astype(F32)
        s3[pl.ds(ch * zpc, zpc)] = total.reshape(zpc, two, tile).astype(BF16)
        for zt in range(ch * zpc, (ch + 1) * zpc):
            d = lax.rem(zt - zl + 2 * nzl - 1 - nzl // 2, nzl) - (nzl // 2 - 1)
            q3[zt] = copy(s3.at[zt], r3.at[zl], q3_s.at[zt], q3_r.at[zl], zdev(d))

            @pl.when(zl != zt)
            def _(zt=zt):
                q3[zt].start()
    r3[zl] = s3[zl]
    for cp in u2:
        cp.wait_recv()
    ototal = o2f[y]
    for i in range(1, ny):
        ototal += o2[i - 1].astype(F32)
    r4[zh, pl.ds(two, ROWS), :] = ototal.astype(BF16)
    for k in range(nzl):
        @pl.when(zl != k)
        def _(k=k):
            copy(s3.at[k], r3.at[k], q3_s.at[k], q3_r.at[k], zdev(1)).wait_recv()
    total = r3[0].astype(F32)
    for k in range(1, nzl):
        total += r3[k].astype(F32)
    r4[zh, pl.ds(0, two), :] = total.astype(BF16)
    q4 = []
    for i in zorder:
        q4.append(go(copy(r4.at[zh], r4.at[zh], q4_s.at[i - 1], q4_r.at[i - 1], zhdev(i))))
    for cp in q4:
        cp.wait_recv()
    total = r4[0].astype(F32)
    for i in range(1, nzh):
        total += r4[i].astype(F32)
    fin_s[...] = total[0:two].reshape(2, ROWS, tile)
    fo[x] = total[two:two + ROWS]
    mine_t = c * nx + x
    fin[mine_t] = fin_s[c]
    q5, q6 = [], []
    q5.append(go(copy(fin_s.at[oc], fin.at[mine_t], q5_s.at[0], q5_r.at[0], other)))
    for i in range(1, nx):
        q5.append(go(copy(fin_s.at[c], fin.at[mine_t], q5_s.at[i], q5_r.at[i], xdev(i, c))))
        q5.append(go(copy(fin_s.at[oc], fin.at[mine_t], q5_s.at[nx + i - 1], q5_r.at[nx + i - 1],
                          xdev(i, oc))))
        q6.append(go(copy(fo.at[x], fo.at[x], q6_s.at[i - 1], q6_r.at[i - 1], xdev(i, c))))
    for cp in q6:
        cp.wait_recv()
    for cp in q5:
        cp.wait_recv()

    scale = 1.0 / math.sqrt(nx * nzh * pts * ngrid)
    total = fo[0]
    for i in range(1, nx):
        total += fo[i]
    go_o[...] = (total * scale)[:, 0:sz.chans]
    dots = jnp.zeros((ROWS, 1), F32)
    for t in range(2 * nx):
        part = fin[t] * scale
        gh_o[:, pl.ds(t * tile, tile)] = part
        dots += jnp.sum(part * wbuf[zl, y, c, :, pl.ds(t * tile, tile)].astype(F32), axis=-1, keepdims=True)
    row = lax.broadcasted_iota(jnp.int32, (ROWS, hid), 0)
    col = lax.broadcasted_iota(jnp.int32, (ROWS, hid), 1)
    gains = jnp.sum(jnp.where(col == row + grd * ROWS, gain_r[...], 0.0), axis=-1, keepdims=True)
    dots = dots / gains
    row = lax.broadcasted_iota(jnp.int32, (ROWS, ROWS), 0)
    col = lax.broadcasted_iota(jnp.int32, (ROWS, ROWS), 1)
    gg_o[...] = jnp.sum(jnp.where(row == col, dots, 0.0), axis=0, keepdims=True)

    for cp in sent:
        cp.wait_send()

    @pl.when(spread)
    def _():
        for d in window:
            wz[d].wait_send()
    for zt in range(nzl):
        @pl.when(zl != zt)
        def _(zt=zt):
            q3[zt].wait_send()


def body(sz, mesh_latent, grid_latent, edges, truth, area, chan_weight, gain, w_hidden, w_out):
    nx, ny, nzl, nzh = sz.x, sz.y, sz.zl, sz.zh
    hid = nzl * ny * 2 * ROWS
    half = hid // 2
    tile = half // nx
    pts, pad, nch = sz.points, sz.pad, sz.chunks
    quarter = pad // nx
    zpc = nzl // nch
    rc = zpc * 2 * ROWS
    win = max(nzl - 1, 1)
    V = pltpu.VMEM

    def sems(*shape):
        return [pltpu.SemaphoreType.DMA(shape)] * 2

    scratch = [
        V((sz.nodes, hid), BF16),
        V((pts, hid), BF16),
        V((3, pts), jnp.int32),
        V((sz.chans, pts), F32),
        V((1, pts), F32),
        V((1, sz.chans), F32),
        V((1, hid), F32),
        V((ROWS, sz.chans), BF16),
        V((nzl, ny, 2, ROWS, hid + pad), BF16),
        V((2, sz.nodes, hid), BF16),
        V((pts, hid), BF16),
        V((2, hid, pts), BF16),
        V((2, hid, pts), BF16),
        V((pts, hid), F32),
        V((pts, hid), F32),
        V((nx, quarter, pts), BF16),
        V((pad, pts), F32),
        V((8, pad), F32),
        V((nzh, nx, quarter, pts), BF16),
        V((nx, quarter, pts), BF16),
        V((nx, quarter, pts), BF16),
        V((2, pts, pad), BF16),
        V((pts, half), BF16),
        V((2, pts, half), BF16),
        V((ny, 2, ROWS, pad), F32),
        V((nch, nx, ny, rc, tile), BF16),
        V((nch, nx - 1, ny, rc, tile), BF16),
        V((nch, ny, rc, tile), F32),
        V((nch, ny, rc, tile), BF16),
        V((nch, ny - 1, rc, tile), BF16),
        V((nzl, 2 * ROWS, tile), BF16),
        V((nzl, 2 * ROWS, tile), BF16),
        V((nzl, ny, ROWS, pad), BF16),
        V((nzl, ny, ROWS, pad), F32),
        V((win, ny, ROWS, pad), BF16),
        V((ny - 1, ROWS, pad), BF16),
        V((ny, ROWS, pad), BF16),
        V((ny, ROWS, pad), F32),
        V((nzh, 3 * ROWS, tile), BF16),
        V((2, ROWS, tile), F32),
        V((2 * nx, ROWS, tile), F32),
        V((nx, ROWS, pad), F32),
        pltpu.SemaphoreType.REGULAR,
        pltpu.SemaphoreType.REGULAR,
        pltpu.SemaphoreType.DMA((9,)),
    ]
    scratch += sems(nzl) + sems(nzl, ny - 1) + sems(nx - 1) + sems(nzl) + sems(2) + sems(4)
    scratch += sems(nx - 1) + sems(nzh - 1) + sems(nx - 1)
    scratch += sems(nch, nx - 1) + sems(nch, ny - 1) + sems(nzl) + sems(nzh - 1)
    scratch += sems(2 * nx - 1) + sems(nx - 1) + sems(win) + sems(ny - 1)
    vmem = pl.BlockSpec(memory_space=pltpu.VMEM)
    outs = pl.pallas_call(
        functools.partial(kernel, sz),
        out_shape=(
            jax.ShapeDtypeStruct((ROWS, hid), F32),
            jax.ShapeDtypeStruct((ROWS, sz.chans), F32),
            jax.ShapeDtypeStruct((1, ROWS), F32),
            jax.ShapeDtypeStruct((sz.chans, pts), F32),
        ),
        in_specs=[pl.BlockSpec(memory_space=pltpu.HBM)] * 9,
        out_specs=(vmem,) * 4,
        scratch_shapes=scratch,
        compiler_params=pltpu.CompilerParams(
            collective_id=0, has_side_effects=True, vmem_limit_bytes=40 * 1024 * 1024),
        cost_estimate=pl.CostEstimate(flops=10**9, bytes_accessed=10**6, transcendentals=10**6),
    )(*[pltpu.with_memory_space_constraint(a, pltpu.HBM) for a in (
        mesh_latent[0], grid_latent[0], edges.T, truth, area[None], chan_weight[None], gain[None],
        w_hidden, w_out)])
    return outs[0], outs[1], outs[2][0], outs[3][None]


def program(mesh, sz):
    return jax.shard_map(
        functools.partial(body, sz),
        mesh=mesh,
        in_specs=(
            P("ens", "grid", None),
            P("ens", "grid", None),
            P("grid", None),
            P(None, "grid"),
            P("grid"),
            P(),
            P(),
            P("grid", None),
            P("grid", None),
        ),
        out_specs=(P("grid", None), P("grid", None), P("grid"), P("ens", None, "grid")),
        check_vma=False,
    )


def solution(mesh):
    return program(mesh, Sizes())
```

```python
import functools
import math
from typing import NamedTuple

import jax
import jax.numpy as jnp
from jax import lax
from jax.experimental import pallas as pl
from jax.experimental.pallas import tpu as pltpu
from jax.sharding import PartitionSpec as P

LN_EPS = 1e-05
F32, BF16 = jnp.float32, jnp.bfloat16
ROWS = 16
NT = (((1,), (1,)), ((), ()))


class Sizes(NamedTuple):
    x: int = 4
    y: int = 4
    zl: int = 8
    zh: int = 4
    points: int = 128
    nodes: int = 64
    chans: int = 100
    pad: int = 128
    chunks: int = 4


def slope(diff):
    return diff * lax.rsqrt(diff * diff + 0.01)


def kernel(sz, mesh_h, grid_h, edges_h, truth_h, area_h, cw_h, gain_h, wh_h, wo_h,
           gh_o, go_o, gg_o, pg_o,
           mesh_r, grid_r, edges_r, truth_r, area_r, cw_r, gain_r, wo_r,
           wbuf, halo, normed, norm_t, act_t, pre, gprime, truth_s, cw_s,
           pall, gb, dp_send, dp_all, dout_s,
           mb, r2, s3, r3, ob, obf, o1, o2, o2s, o2f, r4, fin_s, fin, fo,
           near, far, lo_s,
           xn_s, xn_r, cn_s, cn_r,
           wz_s, wz_r, wy_s, wy_r, wx_s, wx_r, wc_s, wc_r, ha_s, ha_r, tc_s, tc_r,
           p1_s, p1_r, p2_s, p2_r,
           q1_s, q1_r, q2_s, q2_r, q3_s, q3_r, q4_s, q4_r, q5_s, q5_r, q6_s, q6_r,
           u1_s, u1_r, u2_s, u2_r):
    nx, ny, nzl, nzh = sz.x, sz.y, sz.zl, sz.zh
    nz = nzl * nzh
    hid = nzl * ny * 2 * ROWS
    slab = ny * 2 * ROWS
    half = hid // 2
    tile = half // nx
    pts, pad, nch = sz.points, sz.pad, sz.chunks
    sent_rows = -(-sz.chans // ROWS) * ROWS
    two = 2 * ROWS
    zpc = nzl // nch

    ens, grd = lax.axis_index("ens"), lax.axis_index("grid")
    x, zh = lax.div(ens, nzh), lax.rem(ens, nzh)
    c = lax.rem(grd, 2)
    y = lax.rem(lax.div(grd, 2), ny)
    zl = lax.div(grd, 2 * ny)
    z = zh * nzl + zl
    oc = 1 - c
    ngrid = nzl * ny * 2

    def at(x_, y_, z_, c_):
        return (x_ * nzh + lax.div(z_, nzl), (lax.rem(z_, nzl) * ny + y_) * 2 + c_)

    window = []
    for d in range(1, nzl // 2 + 1):
        window.append(d)
        if d < nzl // 2 or nzl == 1:
            window.append(-d)
    window = window[: nzl - 1]

    def zdev(d):
        return at(x, y, lax.rem(z + d + nz, nz), c)

    def zhdev(i):
        return at(x, y, lax.rem(zh + i, nzh) * nzl + zl, c)

    def ydev(i):
        return at(x, lax.rem(y + i, ny), z, c)

    def xdev(i, c_):
        return at(lax.rem(x + i, nx), y, z, c_)

    left = (ens, lax.rem(grd + ngrid - 1, ngrid))
    right = (ens, lax.rem(grd + 1, ngrid))
    other = at(x, y, z, oc)

    def signal(sem, dev):
        pl.semaphore_signal(sem, inc=1, device_id=dev, device_id_type=pl.DeviceIdType.MESH)

    partners = [zdev(d) for d in window] + [zdev(-d) for d in window]
    partners += [ydev(i) for i in range(1, ny)]
    partners += [xdev(i, c) for i in range(1, nx)] + [xdev(i, oc) for i in range(1, nx)]
    partners += [left, right, other]
    barrier = pltpu.get_barrier_semaphore()
    for dev in partners:
        signal(barrier, dev)

    def fetch(k, src, dst):
        cp = pltpu.make_async_copy(src, dst, lo_s.at[k])
        cp.start()
        return cp

    lo_m = [fetch(2, mesh_h, mesh_r), fetch(3, edges_h, edges_r), fetch(4, grid_h, grid_r),
            fetch(5, gain_h, gain_r)]
    lo_t = [fetch(6, truth_h, truth_r), fetch(7, area_h, area_r), fetch(8, cw_h, cw_r)]

    sent = []

    def copy(src, dst, ssem, rsem, dev):
        return pltpu.make_async_remote_copy(
            src_ref=src, dst_ref=dst, send_sem=ssem, recv_sem=rsem,
            device_id=dev, device_id_type=pl.DeviceIdType.MESH)

    def go(cp):
        cp.start()
        sent.append(cp)
        return cp

    odd = lax.rem(zl, 2)
    zb = 2 * x + 1
    spread = jnp.logical_or(odd == 0, zl == zb)

    @pl.when(spread)
    def _():
        wbuf[zl, y, c, :, pl.ds(hid, pad)] = jnp.zeros((ROWS, pad), BF16)
        lo_w = [fetch(0, wh_h, wbuf.at[zl, y, c, :, pl.ds(0, hid)]), fetch(1, wo_h, wo_r)]
        for cp in lo_w:
            cp.wait()
        wbuf[zl, y, c, :, pl.ds(hid, sz.chans)] = wo_r[...]

    pl.semaphore_wait(barrier, len(partners))

    reach = nzl // 2
    signal(near, zdev(reach))
    signal(near, zdev(-reach))

    block = wbuf.at[zl, y, c]
    wz = {d: copy(block, block, wz_s.at[j], wz_r.at[zl], zdev(d)) for j, d in enumerate(window)}

    @pl.when(spread)
    def _():
        for d in window:
            wz[d].start()

    def wz_wait(zk):
        got = wbuf.at[zk, y, c]
        copy(got, got, wz_s.at[0], wz_r.at[zk], zdev(1)).wait_recv()

    def wy_start(zk):
        blk = wbuf.at[zk, y, c]
        return [go(copy(blk, blk, wy_s.at[zk, i - 1], wy_r.at[zk, i - 1], ydev(i)))
                for i in range(1, ny)]

    def wc_start(zk):
        blk = wbuf.at[zk, :, c]
        return go(copy(blk, blk, wc_s.at[zk], wc_r.at[zk], other))

    evens = [0] + [-d for d in window if d % 2 == 0]
    odds = [-d for d in window if d % 2 == 1]
    za = [lax.rem(zl + e + (o - e) * odd + nzl, nzl) for e, o in zip(evens, odds, strict=True)]
    nk = len(za)
    wy = {}

    @pl.when(odd == 1)
    def _():
        wz_wait(za[0])
    wy[0] = wy_start(za[0])

    for cp in lo_m:
        cp.wait()
    local = (edges_r[...] - (grd - 1) * sz.nodes + ngrid * sz.nodes) % (ngrid * sz.nodes)
    node = lax.broadcasted_iota(jnp.int32, (sz.nodes, pts), 0)

    def counts(base):
        total = jnp.zeros((sz.nodes, pts), F32)
        for k in range(3):
            total += jnp.where(local[k:k + 1, :] == node + base, 1.0, 0.0)
        return total.T.astype(BF16)

    agg = jnp.dot(counts(sz.nodes), mesh_r[...], preferred_element_type=F32)

    def wx_start(j):
        blk = wbuf.at[zb, lax.rem(y - j + ny, ny), c]
        for i in range(1, nx):
            go(copy(blk, blk, wx_s.at[i - 1, j], wx_r.at[i - 1, j], xdev(i, c)))

    ha = [go(copy(mesh_h, halo.at[0], ha_s.at[0], ha_r.at[0], right)),
          go(copy(mesh_h, halo.at[1], ha_s.at[1], ha_r.at[1], left))]

    @pl.when(zl != zb)
    def _():
        wz_wait(zb)
    wyb = wy_start(zb)
    wx_start(0)
    for k in range(1, nk):
        wz_wait(za[k])
        wy[k] = wy_start(za[k])
    for j in range(1, ny):
        wyb[j - 1].wait_recv()
        wx_start(j)
    wc_start(zb)
    pl.semaphore_wait(near, 2)
    signal(far, zhdev(1))
    signal(far, zhdev(nzh - 1))

    def slab_in(k):
        for cp in wy[k]:
            cp.wait_recv()
        wc_start(za[k])

    slab_in(0)

    ha[0].wait_recv()
    agg += jnp.dot(counts(0), halo[0], preferred_element_type=F32)
    ha[1].wait_recv()
    agg += jnp.dot(counts(2 * sz.nodes), halo[1], preferred_element_type=F32)
    state = grid_r[...].astype(F32) + agg / 3.0
    center = state - jnp.mean(state, axis=-1, keepdims=True)
    var = jnp.mean(center * center, axis=-1, keepdims=True)
    pre[...] = center * lax.rsqrt(var + LN_EPS) * gain_r[...]
    normed[...] = pre[...].astype(BF16)

    def turn(src, dst):
        def step(k, carry):
            cols = pl.ds(pl.multiple_of(k * slab, slab), slab)
            dst[cols, :] = src[:, cols].astype(F32).T.astype(BF16)
            return carry
        lax.fori_loop(0, nzl, step, 0)

    pre[...] = jnp.zeros((pts, hid), F32)

    def multiply(zk):
        got = wbuf.at[zk, :, oc]
        copy(got, got, wc_s.at[zk], wc_r.at[zk], other).wait_recv()
        cols = pl.ds(pl.multiple_of(zk * slab, slab), slab)
        pre[...] += jnp.dot(
            normed[:, cols], wbuf[zk, :, :, :, pl.ds(0, hid)].reshape(slab, hid),
            preferred_element_type=F32)

    for k in range(1, nk):
        slab_in(k)
    ready = za[:1] + [zb] + za[1:]
    multiply(ready.pop(0))
    multiply(ready.pop(0))
    zx = [2 * lax.rem(x - i + nx, nx) + 1 for i in range(nx)]
    order = [1] + ([nx - 1] if nx > 2 else []) + list(range(2, nx - 1))
    for k, i in enumerate(order):
        for j in range(ny):
            got = wbuf.at[zx[i], lax.rem(y - j + ny, ny), c]
            copy(got, got, wx_s.at[i - 1, j], wx_r.at[i - 1, j], xdev(i, c)).wait_recv()
        wc_start(zx[i])
        multiply(ready.pop(0))
        ready.append(zx[i])
    for zk in ready:
        multiply(zk)

    k0, k1 = 0.7978845608028654, 0.044715
    v = pre[...]
    act = 0.5 * v * (1.0 + jnp.tanh(k0 * (v + k1 * v * v * v)))
    wout = wbuf[:, :, :, :, pl.ds(hid, pad)].reshape(hid, pad)
    pred_t = jnp.dot(act.astype(BF16), wout, preferred_element_type=F32)
    send = pl.ds(0, sent_rows)
    pall[zh, x] = pred_t.T.astype(BF16)
    pl.semaphore_wait(far, 2)
    zorder = [nzh // 2] + [i for i in range(1, nzh) if i != nzh // 2]
    xorder = [nx // 2] + [i for i in range(1, nx) if i != nx // 2]
    p1, p2 = {}, {}
    for i in zorder:
        blk = pall.at[zh, x, send]
        p1[i] = go(copy(blk, blk, p1_s.at[i - 1], p1_r.at[i - 1], zhdev(i)))

    def share(i):
        blk = pall.at[lax.rem(zh - i + nzh, nzh), x, send]
        for j in xorder:
            p2[i, j] = go(copy(blk, blk, p2_s.at[i, j - 1], p2_r.at[i, j - 1], xdev(j, c)))

    share(0)
    me = x * 2 + c
    turn(normed, norm_t.at[me])
    cn = [go(copy(norm_t.at[me], norm_t.at[me], cn_s.at[0], cn_r.at[0], other))]
    xn = {}
    for i in range(1, nx):
        xn[i] = go(copy(norm_t.at[me], norm_t.at[me], xn_s.at[i - 1], xn_r.at[i - 1], xdev(i, c)))
    th = jnp.tanh(k0 * (v + k1 * v * v * v))
    gprime[...] = 0.5 * (1.0 + th) + 0.5 * v * (1.0 - th * th) * (k0 * (1.0 + 3.0 * k1 * v * v))
    pre[...] = 0.5 * v * (1.0 + th)
    turn(pre, act_t.at[c])
    ta = go(copy(act_t.at[c], act_t.at[c], tc_s.at[0], tc_r.at[0], other))
    for cp in lo_t:
        cp.wait()
    truth_s[...] = jnp.zeros_like(truth_s)
    truth_s[pl.ds(0, sz.chans), :] = truth_r[...]
    cw_s[...] = jnp.zeros_like(cw_s)
    cw_s[pl.ds(0, 1), pl.ds(0, sz.chans)] = cw_r[...]
    weight = jnp.broadcast_to(cw_s[pl.ds(0, 1), :], (pad, pad)).T[:, 0:1] * area_r[...]
    mine = pall[zh, x, send].astype(F32)
    own = slope(mine - truth_s[send, :])
    pair = jnp.zeros((sent_rows, pts), F32)

    def add_pairs(total, i):
        zs = lax.rem(zh - i + nzh, nzh)
        total += slope(mine - pall[zs, x, send].astype(F32))
        for j in xorder:
            p2[i, j].wait_recv()
            total += slope(mine - pall[zs, lax.rem(x - j + nx, nx), send].astype(F32))
        return total

    pair = add_pairs(pair, 0)
    for i in zorder[1:]:
        p1[i].wait_recv()
        share(i)
    for i in zorder[1:]:
        pair = add_pairs(pair, i)
    for k in range(1, nx):
        xn[k].wait_recv()
        got = norm_t.at[lax.rem(x - k + nx, nx) * 2 + c]
        cn.append(go(copy(got, got, cn_s.at[k], cn_r.at[k], other)))
    p1[zorder[0]].wait_recv()
    share(zorder[0])
    pair = add_pairs(pair, zorder[0])
    pgrad = weight[0:sent_rows] * (own - pair / (nx * nzh - 1.0))
    pg_o[...] = pgrad[0:sz.chans, :].reshape(sz.chans, 1, pts)
    truth_s[send, :] = pgrad
    if sent_rows < pad:
        truth_s[pl.ds(sent_rows, pad - sent_rows), :] = jnp.zeros((pad - sent_rows, pts), F32)
    gb[c] = truth_s[...].T.astype(BF16)
    tg = go(copy(gb.at[c], gb.at[c], tc_s.at[1], tc_r.at[1], other))

    for which in range(2):
        w = wbuf[pl.ds(which * (nzl // 2), nzl // 2), :, :, :, pl.ds(hid, pad)].reshape(half, pad)
        d_act = lax.dot_general(gb[c], w, NT, preferred_element_type=F32)
        d_pre = (d_act * gprime[:, pl.ds(which * half, half)]).astype(BF16)
        for xx in range(nx):
            dp_send[which, xx] = d_pre[:, xx * tile:(xx + 1) * tile]
    q1 = []
    for i in xorder + [0]:
        to = lax.rem(x + i, nx)
        for k, cc in ((0, c), (1, oc)):
            if i > 0 or k > 0:
                q1.append(go(copy(dp_send.at[cc, to], dp_all.at[me], q1_s.at[2 * i + k],
                                  q1_r.at[2 * i + k], xdev(i, cc))))
    dp_all[me] = dp_send[c, x]
    for cp in cn:
        cp.wait_recv()
    for cp in q1:
        cp.wait_recv()

    q2 = {}
    for ch in range(nch):
        rows = pl.ds(ch * zpc * slab, zpc * slab)
        lhs = jnp.concatenate([norm_t[k, rows, :] for k in range(2 * nx)], axis=1)
        res = jnp.dot(lhs, dp_all[...].reshape(2 * nx * pts, tile), preferred_element_type=F32)
        res = res.astype(BF16).reshape(zpc, ny, two, tile)
        for yy in range(ny):
            mb[ch, yy] = res[:, yy]
        for i in range(1, ny):
            to = lax.rem(y + i, ny)
            q2[ch, i] = go(copy(mb.at[ch, to], r2.at[ch, i - 1], q2_s.at[ch, i - 1],
                                q2_r.at[ch, i - 1], ydev(i)))

    ta.wait_recv()
    tg.wait_recv()

    def out_step(k, carry):
        rows = pl.ds(pl.multiple_of(k * slab, slab), slab)
        lhs = jnp.concatenate([act_t[0, rows, :], act_t[1, rows, :]], axis=1)
        res = jnp.dot(lhs, gb[...].reshape(2 * pts, pad), preferred_element_type=F32)
        dout_s[...] = res.reshape(ny, 2, ROWS, pad)
        part = dout_s[:, c]
        obf[k] = part
        ob[k] = part.astype(BF16)
        return carry

    lax.fori_loop(0, nzl, out_step, 0)
    u1 = []
    for j, d in enumerate(window):
        to = lax.rem(zl + d + nzl, nzl)
        u1.append(go(copy(ob.at[to], o1.at[j], u1_s.at[j], u1_r.at[j], zdev(d))))

    for cp in u1:
        cp.wait_recv()
    total = obf[zl]
    for j in range(len(window)):
        total += o1[j].astype(F32)
    o2f[...] = total
    o2s[...] = total.astype(BF16)
    u2 = []
    for i in range(1, ny):
        to = lax.rem(y + i, ny)
        u2.append(go(copy(o2s.at[to], o2.at[i - 1], u2_s.at[i - 1], u2_r.at[i - 1], ydev(i))))
    q3 = {}
    for ch in range(nch):
        total = mb[ch, y].astype(F32)
        for i in range(1, ny):
            q2[ch, i].wait_recv()
            total += r2[ch, i - 1].astype(F32)
        s3[pl.ds(ch * zpc, zpc)] = total.astype(BF16)
        for zt in range(ch * zpc, (ch + 1) * zpc):
            d = lax.rem(zt - zl + 2 * nzl - 1 - nzl // 2, nzl) - (nzl // 2 - 1)
            q3[zt] = copy(s3.at[zt], r3.at[zl], q3_s.at[zt], q3_r.at[zl], zdev(d))

            @pl.when(zl != zt)
            def _(zt=zt):
                q3[zt].start()
    r3[zl] = s3[zl]
    for cp in u2:
        cp.wait_recv()
    ototal = o2f[y]
    for i in range(1, ny):
        ototal += o2[i - 1].astype(F32)
    r4[zh, pl.ds(two, ROWS), :] = ototal.astype(BF16)
    for k in range(nzl):
        @pl.when(zl != k)
        def _(k=k):
            copy(s3.at[k], r3.at[k], q3_s.at[k], q3_r.at[k], zdev(1)).wait_recv()
    total = r3[0].astype(F32)
    for k in range(1, nzl):
        total += r3[k].astype(F32)
    r4[zh, pl.ds(0, two), :] = total.astype(BF16)
    q4 = []
    for i in zorder:
        q4.append(go(copy(r4.at[zh], r4.at[zh], q4_s.at[i - 1], q4_r.at[i - 1], zhdev(i))))
    for cp in q4:
        cp.wait_recv()
    total = r4[0].astype(F32)
    for i in range(1, nzh):
        total += r4[i].astype(F32)
    fin_s[...] = total[0:two].reshape(2, ROWS, tile)
    fo[x] = total[two:two + ROWS]
    mine_t = c * nx + x
    fin[mine_t] = fin_s[c]
    q5, q6 = [], []
    q5.append(go(copy(fin_s.at[oc], fin.at[mine_t], q5_s.at[0], q5_r.at[0], other)))
    for i in range(1, nx):
        q5.append(go(copy(fin_s.at[c], fin.at[mine_t], q5_s.at[i], q5_r.at[i], xdev(i, c))))
        q5.append(go(copy(fin_s.at[oc], fin.at[mine_t], q5_s.at[nx + i - 1], q5_r.at[nx + i - 1],
                          xdev(i, oc))))
        q6.append(go(copy(fo.at[x], fo.at[x], q6_s.at[i - 1], q6_r.at[i - 1], xdev(i, c))))
    for cp in q6:
        cp.wait_recv()
    for cp in q5:
        cp.wait_recv()

    scale = 1.0 / math.sqrt(nx * nzh * pts * ngrid)
    total = fo[0]
    for i in range(1, nx):
        total += fo[i]
    go_o[...] = (total * scale)[:, 0:sz.chans]
    dots = jnp.zeros((ROWS, 1), F32)
    for t in range(2 * nx):
        part = fin[t] * scale
        gh_o[:, pl.ds(t * tile, tile)] = part
        dots += jnp.sum(part * wbuf[zl, y, c, :, pl.ds(t * tile, tile)].astype(F32), axis=-1, keepdims=True)
    row = lax.broadcasted_iota(jnp.int32, (ROWS, hid), 0)
    col = lax.broadcasted_iota(jnp.int32, (ROWS, hid), 1)
    gains = jnp.sum(jnp.where(col == row + grd * ROWS, gain_r[...], 0.0), axis=-1, keepdims=True)
    dots = dots / gains
    row = lax.broadcasted_iota(jnp.int32, (ROWS, ROWS), 0)
    col = lax.broadcasted_iota(jnp.int32, (ROWS, ROWS), 1)
    gg_o[...] = jnp.sum(jnp.where(row == col, dots, 0.0), axis=0, keepdims=True)

    for cp in sent:
        cp.wait_send()

    @pl.when(spread)
    def _():
        for d in window:
            wz[d].wait_send()
    for zt in range(nzl):
        @pl.when(zl != zt)
        def _(zt=zt):
            q3[zt].wait_send()


def body(sz, mesh_latent, grid_latent, edges, truth, area, chan_weight, gain, w_hidden, w_out):
    nx, ny, nzl, nzh = sz.x, sz.y, sz.zl, sz.zh
    hid = nzl * ny * 2 * ROWS
    half = hid // 2
    tile = half // nx
    pts, pad, nch = sz.points, sz.pad, sz.chunks
    zpc = nzl // nch
    win = max(nzl - 1, 1)
    V = pltpu.VMEM

    def sems(*shape):
        return [pltpu.SemaphoreType.DMA(shape)] * 2

    scratch = [
        V((sz.nodes, hid), BF16),
        V((pts, hid), BF16),
        V((3, pts), jnp.int32),
        V((sz.chans, pts), F32),
        V((1, pts), F32),
        V((1, sz.chans), F32),
        V((1, hid), F32),
        V((ROWS, sz.chans), BF16),
        V((nzl, ny, 2, ROWS, hid + pad), BF16),
        V((2, sz.nodes, hid), BF16),
        V((pts, hid), BF16),
        V((2 * nx, hid, pts), BF16),
        V((2, hid, pts), BF16),
        V((pts, hid), F32),
        V((pts, hid), F32),
        V((pad, pts), F32),
        V((8, pad), F32),
        V((nzh, nx, pad, pts), BF16),
        V((2, pts, pad), BF16),
        V((2, nx, pts, tile), BF16),
        V((2 * nx, pts, tile), BF16),
        V((ny, 2, ROWS, pad), F32),
        V((nch, ny, zpc, 2 * ROWS, tile), BF16),
        V((nch, ny - 1, zpc, 2 * ROWS, tile), BF16),
        V((nzl, 2 * ROWS, tile), BF16),
        V((nzl, 2 * ROWS, tile), BF16),
        V((nzl, ny, ROWS, pad), BF16),
        V((nzl, ny, ROWS, pad), F32),
        V((win, ny, ROWS, pad), BF16),
        V((ny - 1, ROWS, pad), BF16),
        V((ny, ROWS, pad), BF16),
        V((ny, ROWS, pad), F32),
        V((nzh, 3 * ROWS, tile), BF16),
        V((2, ROWS, tile), F32),
        V((2 * nx, ROWS, tile), F32),
        V((nx, ROWS, pad), F32),
        pltpu.SemaphoreType.REGULAR,
        pltpu.SemaphoreType.REGULAR,
        pltpu.SemaphoreType.DMA((9,)),
    ]
    scratch += sems(nx - 1) + sems(nx)
    scratch += sems(nzl) + sems(nzl, ny - 1) + sems(nx - 1, ny) + sems(nzl) + sems(2) + sems(2)
    scratch += sems(nzh - 1) + sems(nzh, nx - 1)
    scratch += sems(2 * nx) + sems(nch, ny - 1) + sems(nzl) + sems(nzh - 1)
    scratch += sems(2 * nx - 1) + sems(nx - 1) + sems(win) + sems(ny - 1)
    vmem = pl.BlockSpec(memory_space=pltpu.VMEM)
    outs = pl.pallas_call(
        functools.partial(kernel, sz),
        out_shape=(
            jax.ShapeDtypeStruct((ROWS, hid), F32),
            jax.ShapeDtypeStruct((ROWS, sz.chans), F32),
            jax.ShapeDtypeStruct((1, ROWS), F32),
            jax.ShapeDtypeStruct((sz.chans, 1, pts), F32),
        ),
        in_specs=[pl.BlockSpec(memory_space=pltpu.HBM)] * 9,
        out_specs=(vmem,) * 4,
        scratch_shapes=scratch,
        compiler_params=pltpu.CompilerParams(
            collective_id=0, has_side_effects=True, vmem_limit_bytes=40 * 1024 * 1024),
        cost_estimate=pl.CostEstimate(flops=10**9, bytes_accessed=10**6, transcendentals=10**6),
    )(*[pltpu.with_memory_space_constraint(a, pltpu.HBM) for a in (
        mesh_latent[0], grid_latent[0], edges.T, truth, area[None], chan_weight[None], gain[None],
        w_hidden, w_out)])
    return outs[0], outs[1], outs[2][0], outs[3].transpose(1, 0, 2)


def program(mesh, sz):
    return jax.shard_map(
        functools.partial(body, sz),
        mesh=mesh,
        in_specs=(
            P("ens", "grid", None),
            P("ens", "grid", None),
            P("grid", None),
            P(None, "grid"),
            P("grid"),
            P(),
            P(),
            P("grid", None),
            P("grid", None),
        ),
        out_specs=(P("grid", None), P("grid", None), P("grid"), P("ens", None, "grid")),
        check_vma=False,
    )


def solution(mesh):
    return program(mesh, Sizes())
```

```python
import functools
import math
from typing import NamedTuple

import jax
import jax.numpy as jnp
from jax import lax
from jax.experimental import pallas as pl
from jax.experimental.pallas import tpu as pltpu
from jax.sharding import PartitionSpec as P

LN_EPS = 1e-05
F32, BF16 = jnp.float32, jnp.bfloat16
ROWS = 16
NT = (((1,), (1,)), ((), ()))


class Sizes(NamedTuple):
    x: int = 4
    y: int = 4
    zl: int = 8
    zh: int = 4
    points: int = 128
    nodes: int = 64
    chans: int = 100
    pad: int = 128
    chunks: int = 4


def slope(diff):
    return diff * lax.rsqrt(diff * diff + 0.01)


def kernel(sz, mesh_h, grid_h, edges_h, truth_h, area_h, cw_h, gain_h, wh_h, wo_h,
           gh_o, go_o, gg_o, pg_o,
           mesh_r, grid_r, edges_r, truth_r, area_r, cw_r, gain_r, wo_r,
           wbuf, halo, normed, norm_t, act_t, pre, gprime, truth_s, cw_s,
           pall, gb, dp_send, dp_all, dout_s,
           mb, r2, s3, r3, ob, obf, o1, o2, o2s, o2f, r4, fin_s, fin, fo,
           near, far, lo_s,
           xn_s, xn_r, cn_s, cn_r,
           wz_s, wz_r, wy_s, wy_r, wx_s, wx_r, wc_s, wc_r, ha_s, ha_r, tc_s, tc_r,
           p1_s, p1_r, p2_s, p2_r,
           q1_s, q1_r, q2_s, q2_r, q3_s, q3_r, q4_s, q4_r, q5_s, q5_r, q6_s, q6_r,
           u1_s, u1_r, u2_s, u2_r):
    nx, ny, nzl, nzh = sz.x, sz.y, sz.zl, sz.zh
    nz = nzl * nzh
    hid = nzl * ny * 2 * ROWS
    slab = ny * 2 * ROWS
    half = hid // 2
    tile = half // nx
    pts, pad, nch = sz.points, sz.pad, sz.chunks
    sent_rows = -(-sz.chans // ROWS) * ROWS
    two = 2 * ROWS
    zpc = nzl // nch

    ens, grd = lax.axis_index("ens"), lax.axis_index("grid")
    x, zh = lax.div(ens, nzh), lax.rem(ens, nzh)
    c = lax.rem(grd, 2)
    y = lax.rem(lax.div(grd, 2), ny)
    zl = lax.div(grd, 2 * ny)
    z = zh * nzl + zl
    oc = 1 - c
    ngrid = nzl * ny * 2

    def at(x_, y_, z_, c_):
        return (x_ * nzh + lax.div(z_, nzl), (lax.rem(z_, nzl) * ny + y_) * 2 + c_)

    window = []
    for d in range(1, nzl // 2 + 1):
        window.append(d)
        if d < nzl // 2 or nzl == 1:
            window.append(-d)
    window = window[: nzl - 1]

    sg = 1 - 2 * c

    def zdev(d):
        return at(x, y, lax.rem(z + d + nz, nz), c)

    def zhdev(i):
        return at(x, y, lax.rem(zh + i, nzh) * nzl + zl, c)

    def ydev(i):
        return at(x, lax.rem(y + i, ny), z, c)

    def xdev(i, c_):
        return at(lax.rem(x + i, nx), y, z, c_)

    left = (ens, lax.rem(grd + ngrid - 1, ngrid))
    right = (ens, lax.rem(grd + 1, ngrid))
    other = at(x, y, z, oc)

    def signal(sem, dev):
        pl.semaphore_signal(sem, inc=1, device_id=dev, device_id_type=pl.DeviceIdType.MESH)

    partners = [zdev(d) for d in window] + [zdev(-d) for d in window]
    partners += [ydev(i) for i in range(1, ny)]
    partners += [xdev(i, c) for i in range(1, nx)] + [xdev(i, oc) for i in range(1, nx)]
    partners += [left, right, other]
    barrier = pltpu.get_barrier_semaphore()
    for dev in partners:
        signal(barrier, dev)

    def fetch(k, src, dst):
        cp = pltpu.make_async_copy(src, dst, lo_s.at[k])
        cp.start()
        return cp

    lo_m = [fetch(2, mesh_h, mesh_r), fetch(3, edges_h, edges_r), fetch(4, grid_h, grid_r),
            fetch(5, gain_h, gain_r)]
    lo_t = [fetch(6, truth_h, truth_r), fetch(7, area_h, area_r), fetch(8, cw_h, cw_r)]

    sent = []

    def copy(src, dst, ssem, rsem, dev):
        return pltpu.make_async_remote_copy(
            src_ref=src, dst_ref=dst, send_sem=ssem, recv_sem=rsem,
            device_id=dev, device_id_type=pl.DeviceIdType.MESH)

    def go(cp):
        cp.start()
        sent.append(cp)
        return cp

    odd = lax.rem(zl, 2)
    zb = 2 * x + 1
    spread = jnp.logical_or(odd == 0, zl == zb)

    @pl.when(spread)
    def _():
        wbuf[zl, y, c, :, pl.ds(hid, pad)] = jnp.zeros((ROWS, pad), BF16)
        lo_w = [fetch(0, wh_h, wbuf.at[zl, y, c, :, pl.ds(0, hid)]), fetch(1, wo_h, wo_r)]
        for cp in lo_w:
            cp.wait()
        wbuf[zl, y, c, :, pl.ds(hid, sz.chans)] = wo_r[...]

    pl.semaphore_wait(barrier, len(partners))

    reach = nzl // 2
    signal(near, zdev(reach))
    signal(near, zdev(-reach))

    block = wbuf.at[zl, y, c]
    wz = {d: copy(block, block, wz_s.at[j], wz_r.at[zl], zdev(sg * d)) for j, d in enumerate(window)}

    @pl.when(spread)
    def _():
        for d in window:
            wz[d].start()

    def wz_wait(zk):
        got = wbuf.at[zk, y, c]
        copy(got, got, wz_s.at[0], wz_r.at[zk], zdev(1)).wait_recv()

    def wy_start(zk):
        blk = wbuf.at[zk, y, c]
        return [go(copy(blk, blk, wy_s.at[zk, i - 1], wy_r.at[zk, i - 1], ydev(i)))
                for i in range(1, ny)]

    def wc_start(zk):
        blk = wbuf.at[zk, :, c]
        return go(copy(blk, blk, wc_s.at[zk], wc_r.at[zk], other))

    evens = [0] + [-d for d in window if d % 2 == 0]
    odds = [-d for d in window if d % 2 == 1]
    za = [lax.rem(zl + sg * (e + (o - e) * odd) + nzl, nzl) for e, o in zip(evens, odds, strict=True)]
    nk = len(za)
    wy = {}

    @pl.when(odd == 1)
    def _():
        wz_wait(za[0])
    wy[0] = wy_start(za[0])

    for cp in lo_m:
        cp.wait()
    local = (edges_r[...] - (grd - 1) * sz.nodes + ngrid * sz.nodes) % (ngrid * sz.nodes)
    node = lax.broadcasted_iota(jnp.int32, (sz.nodes, pts), 0)

    def counts(base):
        total = jnp.zeros((sz.nodes, pts), F32)
        for k in range(3):
            total += jnp.where(local[k:k + 1, :] == node + base, 1.0, 0.0)
        return total.T.astype(BF16)

    agg = jnp.dot(counts(sz.nodes), mesh_r[...], preferred_element_type=F32)

    def wx_start(j):
        blk = wbuf.at[zb, lax.rem(y - j + ny, ny), c]
        for i in range(1, nx):
            go(copy(blk, blk, wx_s.at[i - 1, j], wx_r.at[i - 1, j], xdev(i, c)))

    ha = [go(copy(mesh_h, halo.at[0], ha_s.at[0], ha_r.at[0], right)),
          go(copy(mesh_h, halo.at[1], ha_s.at[1], ha_r.at[1], left))]

    @pl.when(zl != zb)
    def _():
        wz_wait(zb)
    wyb = wy_start(zb)
    wx_start(0)
    for k in range(1, nk):
        wz_wait(za[k])
        wy[k] = wy_start(za[k])
    for j in range(1, ny):
        wyb[j - 1].wait_recv()
        wx_start(j)
    wc_start(zb)
    pl.semaphore_wait(near, 2)
    signal(far, zhdev(1))
    signal(far, zhdev(nzh - 1))

    def slab_in(k):
        for cp in wy[k]:
            cp.wait_recv()
        wc_start(za[k])

    slab_in(0)

    ha[0].wait_recv()
    agg += jnp.dot(counts(0), halo[0], preferred_element_type=F32)
    ha[1].wait_recv()
    agg += jnp.dot(counts(2 * sz.nodes), halo[1], preferred_element_type=F32)
    state = grid_r[...].astype(F32) + agg / 3.0
    center = state - jnp.mean(state, axis=-1, keepdims=True)
    var = jnp.mean(center * center, axis=-1, keepdims=True)
    pre[...] = center * lax.rsqrt(var + LN_EPS) * gain_r[...]
    normed[...] = pre[...].astype(BF16)

    def turn(src, dst):
        def step(k, carry):
            cols = pl.ds(pl.multiple_of(k * slab, slab), slab)
            dst[cols, :] = src[:, cols].astype(F32).T.astype(BF16)
            return carry
        lax.fori_loop(0, nzl, step, 0)

    pre[...] = jnp.zeros((pts, hid), F32)

    def multiply(zk):
        got = wbuf.at[zk, :, oc]
        copy(got, got, wc_s.at[zk], wc_r.at[zk], other).wait_recv()
        cols = pl.ds(pl.multiple_of(zk * slab, slab), slab)
        pre[...] += jnp.dot(
            normed[:, cols], wbuf[zk, :, :, :, pl.ds(0, hid)].reshape(slab, hid),
            preferred_element_type=F32)

    for k in range(1, nk):
        slab_in(k)
    ready = za[:1] + [zb] + za[1:]
    multiply(ready.pop(0))
    multiply(ready.pop(0))
    zx = [2 * lax.rem(x - i + nx, nx) + 1 for i in range(nx)]
    order = [1] + ([nx - 1] if nx > 2 else []) + list(range(2, nx - 1))
    for k, i in enumerate(order):
        for j in range(ny):
            got = wbuf.at[zx[i], lax.rem(y - j + ny, ny), c]
            copy(got, got, wx_s.at[i - 1, j], wx_r.at[i - 1, j], xdev(i, c)).wait_recv()
        wc_start(zx[i])
        multiply(ready.pop(0))
        ready.append(zx[i])
    for zk in ready:
        multiply(zk)

    k0, k1 = 0.7978845608028654, 0.044715
    v = pre[...]
    act = 0.5 * v * (1.0 + jnp.tanh(k0 * (v + k1 * v * v * v)))
    wout = wbuf[:, :, :, :, pl.ds(hid, pad)].reshape(hid, pad)
    pred_t = jnp.dot(act.astype(BF16), wout, preferred_element_type=F32)
    send = pl.ds(0, sent_rows)
    pall[zh, x] = pred_t.T.astype(BF16)
    pl.semaphore_wait(far, 2)
    zorder = [nzh // 2] + [i for i in range(1, nzh) if i != nzh // 2]
    xorder = [nx // 2] + [i for i in range(1, nx) if i != nx // 2]
    p1, p2 = {}, {}
    for i in zorder:
        blk = pall.at[zh, x, send]
        p1[i] = go(copy(blk, blk, p1_s.at[i - 1], p1_r.at[i - 1], zhdev(i)))

    def share(i):
        blk = pall.at[lax.rem(zh - i + nzh, nzh), x, send]
        for j in xorder:
            p2[i, j] = go(copy(blk, blk, p2_s.at[i, j - 1], p2_r.at[i, j - 1], xdev(j, c)))

    share(0)
    me = x * 2 + c
    turn(normed, norm_t.at[me])
    cn = [go(copy(norm_t.at[me], norm_t.at[me], cn_s.at[0], cn_r.at[0], other))]
    xn = {}
    for i in range(1, nx):
        xn[i] = go(copy(norm_t.at[me], norm_t.at[me], xn_s.at[i - 1], xn_r.at[i - 1], xdev(i, c)))
    th = jnp.tanh(k0 * (v + k1 * v * v * v))
    gprime[...] = 0.5 * (1.0 + th) + 0.5 * v * (1.0 - th * th) * (k0 * (1.0 + 3.0 * k1 * v * v))
    pre[...] = 0.5 * v * (1.0 + th)
    turn(pre, act_t.at[c])
    ta = go(copy(act_t.at[c], act_t.at[c], tc_s.at[0], tc_r.at[0], other))
    for cp in lo_t:
        cp.wait()
    truth_s[...] = jnp.zeros_like(truth_s)
    truth_s[pl.ds(0, sz.chans), :] = truth_r[...]
    cw_s[...] = jnp.zeros_like(cw_s)
    cw_s[pl.ds(0, 1), pl.ds(0, sz.chans)] = cw_r[...]
    weight = jnp.broadcast_to(cw_s[pl.ds(0, 1), :], (pad, pad)).T[:, 0:1] * area_r[...]
    mine = pall[zh, x, send].astype(F32)
    own = slope(mine - truth_s[send, :])
    pair = jnp.zeros((sent_rows, pts), F32)

    def add_pairs(total, i):
        zs = lax.rem(zh - i + nzh, nzh)
        total += slope(mine - pall[zs, x, send].astype(F32))
        for j in xorder:
            p2[i, j].wait_recv()
            total += slope(mine - pall[zs, lax.rem(x - j + nx, nx), send].astype(F32))
        return total

    pair = add_pairs(pair, 0)
    for i in zorder[1:]:
        p1[i].wait_recv()
        share(i)
    for i in zorder[1:]:
        pair = add_pairs(pair, i)
    for k in range(1, nx):
        xn[k].wait_recv()
        got = norm_t.at[lax.rem(x - k + nx, nx) * 2 + c]
        cn.append(go(copy(got, got, cn_s.at[k], cn_r.at[k], other)))
    p1[zorder[0]].wait_recv()
    share(zorder[0])
    pair = add_pairs(pair, zorder[0])
    pgrad = weight[0:sent_rows] * (own - pair / (nx * nzh - 1.0))
    pg_o[...] = pgrad[0:sz.chans, :].reshape(sz.chans, 1, pts)
    truth_s[send, :] = pgrad
    if sent_rows < pad:
        truth_s[pl.ds(sent_rows, pad - sent_rows), :] = jnp.zeros((pad - sent_rows, pts), F32)
    gb[c] = truth_s[...].T.astype(BF16)
    tg = go(copy(gb.at[c], gb.at[c], tc_s.at[1], tc_r.at[1], other))

    for which in range(2):
        w = wbuf[pl.ds(which * (nzl // 2), nzl // 2), :, :, :, pl.ds(hid, pad)].reshape(half, pad)
        d_act = lax.dot_general(gb[c], w, NT, preferred_element_type=F32)
        d_pre = (d_act * gprime[:, pl.ds(which * half, half)]).astype(BF16)
        for xx in range(nx):
            dp_send[which, xx] = d_pre[:, xx * tile:(xx + 1) * tile]
    q1 = []
    for i in xorder + [0]:
        to = lax.rem(x + i, nx)
        for k, cc in ((0, c), (1, oc)):
            if i > 0 or k > 0:
                q1.append(go(copy(dp_send.at[cc, to], dp_all.at[me], q1_s.at[2 * i + k],
                                  q1_r.at[2 * i + k], xdev(i, cc))))
    dp_all[me] = dp_send[c, x]
    for cp in cn:
        cp.wait_recv()
    for cp in q1:
        cp.wait_recv()

    q2 = {}
    for ch in range(nch):
        rows = pl.ds(ch * zpc * slab, zpc * slab)
        lhs = jnp.concatenate([norm_t[k, rows, :] for k in range(2 * nx)], axis=1)
        res = jnp.dot(lhs, dp_all[...].reshape(2 * nx * pts, tile), preferred_element_type=F32)
        res = res.astype(BF16).reshape(zpc, ny, two, tile)
        for yy in range(ny):
            mb[ch, yy] = res[:, yy]
        for i in range(1, ny):
            to = lax.rem(y + i, ny)
            q2[ch, i] = go(copy(mb.at[ch, to], r2.at[ch, i - 1], q2_s.at[ch, i - 1],
                                q2_r.at[ch, i - 1], ydev(i)))

    ta.wait_recv()
    tg.wait_recv()

    def out_step(k, carry):
        rows = pl.ds(pl.multiple_of(k * slab, slab), slab)
        lhs = jnp.concatenate([act_t[0, rows, :], act_t[1, rows, :]], axis=1)
        res = jnp.dot(lhs, gb[...].reshape(2 * pts, pad), preferred_element_type=F32)
        dout_s[...] = res.reshape(ny, 2, ROWS, pad)
        part = dout_s[:, c]
        obf[k] = part
        ob[k] = part.astype(BF16)
        return carry

    lax.fori_loop(0, nzl, out_step, 0)
    u1 = []
    for j, d in enumerate(window):
        to = lax.rem(zl + sg * d + nzl, nzl)
        u1.append(go(copy(ob.at[to], o1.at[j], u1_s.at[j], u1_r.at[j], zdev(sg * d))))

    for cp in u1:
        cp.wait_recv()
    total = obf[zl]
    for j in range(len(window)):
        total += o1[j].astype(F32)
    o2f[...] = total
    o2s[...] = total.astype(BF16)
    u2 = []
    for i in range(1, ny):
        to = lax.rem(y + i, ny)
        u2.append(go(copy(o2s.at[to], o2.at[i - 1], u2_s.at[i - 1], u2_r.at[i - 1], ydev(i))))
    q3 = {}
    for ch in range(nch):
        total = mb[ch, y].astype(F32)
        for i in range(1, ny):
            q2[ch, i].wait_recv()
            total += r2[ch, i - 1].astype(F32)
        s3[pl.ds(ch * zpc, zpc)] = total.astype(BF16)
        for zt in range(ch * zpc, (ch + 1) * zpc):
            d = lax.rem(sg * (zt - zl) + 2 * nzl - 1 - nzl // 2, nzl) - (nzl // 2 - 1)
            q3[zt] = copy(s3.at[zt], r3.at[zl], q3_s.at[zt], q3_r.at[zl], zdev(sg * d))

            @pl.when(zl != zt)
            def _(zt=zt):
                q3[zt].start()
    r3[zl] = s3[zl]
    for cp in u2:
        cp.wait_recv()
    ototal = o2f[y]
    for i in range(1, ny):
        ototal += o2[i - 1].astype(F32)
    r4[zh, pl.ds(two, ROWS), :] = ototal.astype(BF16)
    for k in range(nzl):
        @pl.when(zl != k)
        def _(k=k):
            copy(s3.at[k], r3.at[k], q3_s.at[k], q3_r.at[k], zdev(1)).wait_recv()
    total = r3[0].astype(F32)
    for k in range(1, nzl):
        total += r3[k].astype(F32)
    r4[zh, pl.ds(0, two), :] = total.astype(BF16)
    q4 = []
    for i in zorder:
        q4.append(go(copy(r4.at[zh], r4.at[zh], q4_s.at[i - 1], q4_r.at[i - 1], zhdev(i))))
    for cp in q4:
        cp.wait_recv()
    total = r4[0].astype(F32)
    for i in range(1, nzh):
        total += r4[i].astype(F32)
    fin_s[...] = total[0:two].reshape(2, ROWS, tile)
    fo[x] = total[two:two + ROWS]
    mine_t = c * nx + x
    fin[mine_t] = fin_s[c]
    q5, q6 = [], []
    q5.append(go(copy(fin_s.at[oc], fin.at[mine_t], q5_s.at[0], q5_r.at[0], other)))
    for i in range(1, nx):
        q5.append(go(copy(fin_s.at[c], fin.at[mine_t], q5_s.at[i], q5_r.at[i], xdev(i, c))))
        q5.append(go(copy(fin_s.at[oc], fin.at[mine_t], q5_s.at[nx + i - 1], q5_r.at[nx + i - 1],
                          xdev(i, oc))))
        q6.append(go(copy(fo.at[x], fo.at[x], q6_s.at[i - 1], q6_r.at[i - 1], xdev(i, c))))
    for cp in q6:
        cp.wait_recv()
    for cp in q5:
        cp.wait_recv()

    scale = 1.0 / math.sqrt(nx * nzh * pts * ngrid)
    total = fo[0]
    for i in range(1, nx):
        total += fo[i]
    go_o[...] = (total * scale)[:, 0:sz.chans]
    dots = jnp.zeros((ROWS, 1), F32)
    for t in range(2 * nx):
        part = fin[t] * scale
        gh_o[:, pl.ds(t * tile, tile)] = part
        dots += jnp.sum(part * wbuf[zl, y, c, :, pl.ds(t * tile, tile)].astype(F32), axis=-1, keepdims=True)
    row = lax.broadcasted_iota(jnp.int32, (ROWS, hid), 0)
    col = lax.broadcasted_iota(jnp.int32, (ROWS, hid), 1)
    gains = jnp.sum(jnp.where(col == row + grd * ROWS, gain_r[...], 0.0), axis=-1, keepdims=True)
    dots = dots / gains
    row = lax.broadcasted_iota(jnp.int32, (ROWS, ROWS), 0)
    col = lax.broadcasted_iota(jnp.int32, (ROWS, ROWS), 1)
    gg_o[...] = jnp.sum(jnp.where(row == col, dots, 0.0), axis=0, keepdims=True)

    for cp in sent:
        cp.wait_send()

    @pl.when(spread)
    def _():
        for d in window:
            wz[d].wait_send()
    for zt in range(nzl):
        @pl.when(zl != zt)
        def _(zt=zt):
            q3[zt].wait_send()


def body(sz, mesh_latent, grid_latent, edges, truth, area, chan_weight, gain, w_hidden, w_out):
    nx, ny, nzl, nzh = sz.x, sz.y, sz.zl, sz.zh
    hid = nzl * ny * 2 * ROWS
    half = hid // 2
    tile = half // nx
    pts, pad, nch = sz.points, sz.pad, sz.chunks
    zpc = nzl // nch
    win = max(nzl - 1, 1)
    V = pltpu.VMEM

    def sems(*shape):
        return [pltpu.SemaphoreType.DMA(shape)] * 2

    scratch = [
        V((sz.nodes, hid), BF16),
        V((pts, hid), BF16),
        V((3, pts), jnp.int32),
        V((sz.chans, pts), F32),
        V((1, pts), F32),
        V((1, sz.chans), F32),
        V((1, hid), F32),
        V((ROWS, sz.chans), BF16),
        V((nzl, ny, 2, ROWS, hid + pad), BF16),
        V((2, sz.nodes, hid), BF16),
        V((pts, hid), BF16),
        V((2 * nx, hid, pts), BF16),
        V((2, hid, pts), BF16),
        V((pts, hid), F32),
        V((pts, hid), F32),
        V((pad, pts), F32),
        V((8, pad), F32),
        V((nzh, nx, pad, pts), BF16),
        V((2, pts, pad), BF16),
        V((2, nx, pts, tile), BF16),
        V((2 * nx, pts, tile), BF16),
        V((ny, 2, ROWS, pad), F32),
        V((nch, ny, zpc, 2 * ROWS, tile), BF16),
        V((nch, ny - 1, zpc, 2 * ROWS, tile), BF16),
        V((nzl, 2 * ROWS, tile), BF16),
        V((nzl, 2 * ROWS, tile), BF16),
        V((nzl, ny, ROWS, pad), BF16),
        V((nzl, ny, ROWS, pad), F32),
        V((win, ny, ROWS, pad), BF16),
        V((ny - 1, ROWS, pad), BF16),
        V((ny, ROWS, pad), BF16),
        V((ny, ROWS, pad), F32),
        V((nzh, 3 * ROWS, tile), BF16),
        V((2, ROWS, tile), F32),
        V((2 * nx, ROWS, tile), F32),
        V((nx, ROWS, pad), F32),
        pltpu.SemaphoreType.REGULAR,
        pltpu.SemaphoreType.REGULAR,
        pltpu.SemaphoreType.DMA((9,)),
    ]
    scratch += sems(nx - 1) + sems(nx)
    scratch += sems(nzl) + sems(nzl, ny - 1) + sems(nx - 1, ny) + sems(nzl) + sems(2) + sems(2)
    scratch += sems(nzh - 1) + sems(nzh, nx - 1)
    scratch += sems(2 * nx) + sems(nch, ny - 1) + sems(nzl) + sems(nzh - 1)
    scratch += sems(2 * nx - 1) + sems(nx - 1) + sems(win) + sems(ny - 1)
    vmem = pl.BlockSpec(memory_space=pltpu.VMEM)
    outs = pl.pallas_call(
        functools.partial(kernel, sz),
        out_shape=(
            jax.ShapeDtypeStruct((ROWS, hid), F32),
            jax.ShapeDtypeStruct((ROWS, sz.chans), F32),
            jax.ShapeDtypeStruct((1, ROWS), F32),
            jax.ShapeDtypeStruct((sz.chans, 1, pts), F32),
        ),
        in_specs=[pl.BlockSpec(memory_space=pltpu.HBM)] * 9,
        out_specs=(vmem,) * 4,
        scratch_shapes=scratch,
        compiler_params=pltpu.CompilerParams(
            collective_id=0, has_side_effects=True, vmem_limit_bytes=40 * 1024 * 1024),
        cost_estimate=pl.CostEstimate(flops=10**9, bytes_accessed=10**6, transcendentals=10**6),
    )(*[pltpu.with_memory_space_constraint(a, pltpu.HBM) for a in (
        mesh_latent[0], grid_latent[0], edges.T, truth, area[None], chan_weight[None], gain[None],
        w_hidden, w_out)])
    return outs[0], outs[1], outs[2][0], outs[3].transpose(1, 0, 2)


def program(mesh, sz):
    return jax.shard_map(
        functools.partial(body, sz),
        mesh=mesh,
        in_specs=(
            P("ens", "grid", None),
            P("ens", "grid", None),
            P("grid", None),
            P(None, "grid"),
            P("grid"),
            P(),
            P(),
            P("grid", None),
            P("grid", None),
        ),
        out_specs=(P("grid", None), P("grid", None), P("grid"), P("ens", None, "grid")),
        check_vma=False,
    )


def solution(mesh):
    return program(mesh, Sizes())
```
